512 devices in a mesh: facet: 64 (over z, y), pol: 4 (over x), tm: 2 (over core).
Axes of the slice: x: 4, y: 4, z: 16, core: 2. Of those that a mesh axis runs over, the one named last changes fastest.
Arguments:
- tile_spectral_lines: bfloat16 [64, 4, 2, 64, 4096], P('facet', 'pol', None, 'tm'), may hold values from -6 to 6
- taper_leading_axis: bfloat16 [64, 2, 128, 512], P('facet', 'tm'), may hold values from -0.25 to 0.25
- taper_trailing_axis: bfloat16 [64, 2, 128, 512], P('facet', 'tm'), may hold values from -0.25 to 0.25
- depth_layer_factors: bfloat16 [64, 2, 2, 128], P('facet', 'tm'), may hold values from -4 to 4
- measured_correlations: float32 [64, 8, 2, 128], P('facet', None, 'tm', 'pol'), may hold values from -6 to 6
- visibility_groups_table: int32 [64, 2, 3, 8], P('facet', 'tm'), may hold values from 0 to 130815, as said below
- antenna_links: int32 [2, 130816], replicated, may hold values from 0 to 511, as said below
- complex_receiver_factors: float32 [256, 4, 512], replicated, may hold values from -5 to 5
Outputs:
- residual: float32 [64, 8, 2, 128], P('facet', None, 'tm', 'pol')
- gain_grad: float32 [512, 1024], P(('facet', 'pol', 'tm'))
The draws below stay inside these ranges and needn't reach their ends.
Inputs may be any that keep to these rules, and one draw needn't show every extreme that they name: `visibility_groups_table`: for each subgrid and owner, every block has a channel below 256, a count of 1 or more, and baselines offset to offset + count - 1 below 130816; the counts of one owner sum to at most 128, and some owner reaches 128 in every draw. `antenna_links`: each baseline joins two different stations.
All inputs are finite; a program needn't handle non-finite values.
Results may differ from the reference program's by a relative error of at most 0.012.
Values may be sent and summed in bfloat16 or wider, within the bound.
No kernel may reach another device: no remote copies, remote signals or barrier semaphores. Data moves between devices by JAX's collectives and lax.ppermute only.
A program may use at most 192 MiB of HBM per device.

```python
import math
import jax
import jax.numpy as jnp
import numpy as np
from jax import lax

FGRID = 8
NF = 64
FS = 4096
MC = 64
SG = 512
NPOL = 4
NW = 2
NSUB = 64
TMO = 2
VT = 128
NBLK = 8
NCH = 256
NST = 512
NBASE = 130816


def draw_visibility_groups_table(key, part):
    subkeys = jax.random.split(jax.random.fold_in(key, 4101), 5)
    owners_all = NSUB * TMO
    raw_draw = jax.random.randint(subkeys[0], (owners_all,), 0, VT + 1)
    base_load = VT // 16
    owner_loads = base_load + raw_draw * raw_draw * (VT - base_load) // (VT * VT)
    chosen = jax.random.randint(subkeys[1], (), 0, owners_all)
    owner_loads = jnp.where(jnp.arange(owners_all) == chosen, VT, owner_loads)
    weights = jax.random.randint(subkeys[2], (owners_all, NBLK), 1, 17)
    spare_load = owner_loads - NBLK
    amounts = 1 + spare_load[:, None] * weights // jnp.sum(weights, axis=1, keepdims=True)
    amounts = amounts.at[:, NBLK - 1].set(owner_loads - jnp.sum(amounts[:, :NBLK - 1], axis=1))
    channels = jax.random.randint(subkeys[3], (owners_all, NBLK), 0, NCH)
    offsets = jax.random.randint(subkeys[4], (owners_all, NBLK), 0, NBASE - VT + 1)
    block_table = jnp.stack([channels, offsets, amounts], axis=1)
    return block_table.reshape(NSUB, TMO, 3, NBLK).astype(jnp.int32)


def draw_antenna_links(key, part):
    subkeys = jax.random.split(jax.random.fold_in(key, 7723), 2)
    antenna_left = jax.random.randint(subkeys[0], (NBASE,), 0, NST)
    step_ahead = jax.random.randint(subkeys[1], (NBASE,), 1, NST)
    antenna_right = (antenna_left + step_ahead) % NST
    return jnp.stack([antenna_left, antenna_right]).astype(jnp.int32)


def levels(key, dims, cuts, low, high):
    factor_of, own = 1.0, jax.random.fold_in(key, 6)
    for dim, blocks in cuts:
        steps = jnp.exp(jax.random.uniform(jax.random.fold_in(own, dim), (blocks,), jnp.float32, low / len(cuts), high / len(cuts)))
        factor_of = factor_of * jnp.repeat(steps, dims[dim] // blocks).reshape([-1 if axis == dim else 1 for axis in range(len(dims))])
    return factor_of


def noise(own_key, extent, width, bound, cuts=(), held_as=jnp.bfloat16):
    gain = levels(own_key, extent, cuts, -0.22, 0.18) if cuts else 1.0
    drawn = jax.random.normal(own_key, extent, jnp.float32) * width * gain
    return jnp.minimum(jnp.maximum(drawn, -bound), bound).astype(held_as)


def setup_inputs(seed: int = 0) -> dict:
    keys = jax.random.split(jax.random.key(seed), 9)
    tile_spectral_lines = noise(keys[0], (NF, NPOL, 2, MC, FS), 1.0, 6.0, ((0, 64), (1, 4), (3, 2)))
    taper_leading_axis = noise(keys[1], (NSUB, TMO, VT, SG), SG ** -0.5, 0.25, ((0, 64), (1, 2)))
    taper_trailing_axis = noise(keys[2], (NSUB, TMO, VT, SG), SG ** -0.5, 0.25, ((0, 64), (1, 2)))
    depth_layer_factors = noise(keys[3], (NSUB, TMO, NW, VT), NW ** -0.5, 4.0, ((0, 64), (1, 2)))
    measured_correlations = noise(keys[4], (NSUB, 2 * NPOL, TMO, VT), 1.0, 6.0, ((0, 64), (2, 2), (3, 4)), jnp.float32)
    visibility_groups_table = draw_visibility_groups_table(jax.random.fold_in(keys[8], 71), 0)
    antenna_links = draw_antenna_links(jax.random.fold_in(keys[8], 71), 0)
    complex_receiver_factors = noise(keys[7], (NCH, 4, NST), 0.8, 5.0, (), jnp.float32)
    return dict(tile_spectral_lines=tile_spectral_lines, taper_leading_axis=taper_leading_axis, taper_trailing_axis=taper_trailing_axis, depth_layer_factors=depth_layer_factors, measured_correlations=measured_correlations, visibility_groups_table=visibility_groups_table, antenna_links=antenna_links, complex_receiver_factors=complex_receiver_factors)


w_chirp = 0.37
grad_scale = 0.1
feed_first = np.array([0, 0, 1, 1])
feed_second = np.array([0, 1, 0, 1])

def dft_table(length):
    indices = jnp.arange(length, dtype=jnp.int32)
    product = indices[:, None] * indices[None, :] % length
    angles = 2.0 * math.pi / length * product.astype(jnp.float32)
    factor = 1.0 / math.sqrt(length)
    return ((jnp.cos(angles) * factor).astype(jnp.bfloat16), (jnp.sin(angles) * factor).astype(jnp.bfloat16))

def chirp_phase(first_row, row_total, side_cells):
    across = (first_row + jnp.arange(row_total, dtype=jnp.int32) - side_cells // 2).astype(jnp.float32)
    downward = (jnp.arange(side_cells, dtype=jnp.int32) - side_cells // 2).astype(jnp.float32)
    return w_chirp * (across[:, None] * across[:, None] + downward[None, :] * downward[None, :]) / float(side_cells * side_cells)

def make_planes(sub_real, sub_imag, phase_grid, layers):
    planes_list = []
    for plane_index in range(layers):
        angles = 2.0 * math.pi * plane_index * phase_grid
        cosine = jnp.cos(angles)
        sine_part = jnp.sin(angles)
        planes_list.append(jnp.stack([sub_real * cosine - sub_imag * sine_part, sub_real * sine_part + sub_imag * cosine]).astype(jnp.bfloat16))
    return jnp.stack(planes_list)

def decode_slots(block_table, slot_index):
    channels = block_table[..., 0, :]
    offsets = block_table[..., 1, :]
    amounts = block_table[..., 2, :]
    starts = (jnp.cumsum(amounts, axis=-1) - amounts).astype(jnp.int32)
    relative = (slot_index[:, None] - starts[..., None, :]).astype(jnp.int32)
    member = ((relative >= 0) & (relative < amounts[..., None, :])).astype(jnp.int32)
    slot_live = lax.optimization_barrier(jnp.sum(member, axis=-1)).astype(jnp.int32)
    channel = lax.optimization_barrier(jnp.sum(member * channels[..., None, :], axis=-1)).astype(jnp.int32)
    antenna_couple = lax.optimization_barrier(jnp.sum(member * (offsets[..., None, :] + relative), axis=-1)).astype(jnp.int32)
    return (slot_live, channel, antenna_couple)

def model_terms(pred_re, pred_im, obs_re, obs_im, gain_first, gain_second, slot_live):
    first_re = gain_first[..., 2 * feed_first]
    first_im = gain_first[..., 2 * feed_first + 1]
    second_re = gain_second[..., 2 * feed_second]
    second_im = gain_second[..., 2 * feed_second + 1]
    both_re = first_re * second_re + first_im * second_im
    both_im = first_im * second_re - first_re * second_im
    model_re = both_re * pred_re - both_im * pred_im
    model_im = both_re * pred_im + both_im * pred_re
    alive_mask = slot_live.astype(jnp.float32)[..., None]
    resid_re = alive_mask * (obs_re - model_re)
    resid_im = alive_mask * (obs_im - model_im)
    cross_re = second_re * pred_re + second_im * pred_im
    cross_im = second_im * pred_re - second_re * pred_im
    lead_re = -(resid_re * cross_re - resid_im * cross_im)
    lead_im = -(resid_re * cross_im + resid_im * cross_re)
    along_re = first_re * pred_re - first_im * pred_im
    along_im = first_re * pred_im + first_im * pred_re
    trail_re = -(resid_re * along_re + resid_im * along_im)
    trail_im = -(resid_re * along_im - resid_im * along_re)
    leading = jnp.stack([lead_re[..., 0] + lead_re[..., 1], lead_im[..., 0] + lead_im[..., 1], lead_re[..., 2] + lead_re[..., 3], lead_im[..., 2] + lead_im[..., 3]], axis=-1)
    trailing = jnp.stack([trail_re[..., 0] + trail_re[..., 2], trail_im[..., 0] + trail_im[..., 2], trail_re[..., 1] + trail_re[..., 3], trail_im[..., 1] + trail_im[..., 3]], axis=-1)
    return (resid_re, resid_im, leading, trailing)

def real_dot(left_side, right_side):
    return jnp.dot(left_side.astype(jnp.float32), right_side.astype(jnp.float32), precision=lax.Precision.HIGHEST)

def degrid_reference(layers, rows_u, rows_v, weights_w):
    spread_v = jnp.einsum('wcuv,nv->wcun', layers.astype(jnp.float32), rows_v.astype(jnp.float32), precision=lax.Precision.HIGHEST)
    along_u = lax.optimization_barrier(jnp.sum(spread_v * jnp.transpose(rows_u).astype(jnp.float32)[None, None], axis=2))
    return lax.optimization_barrier(jnp.sum(along_u * weights_w.astype(jnp.float32)[:, None, :], axis=0))

def reference(tile_spectral_lines, taper_leading_axis, taper_trailing_axis, depth_layer_factors, measured_correlations, visibility_groups_table, antenna_links, complex_receiver_factors):
    source = tile_spectral_lines.astype(jnp.float32)
    spectrum = jnp.fft.fft(source[:, :, 0] + 1j * source[:, :, 1], axis=-1)[..., :NSUB * MC] / math.sqrt(FS)
    contrib_re = jnp.real(spectrum).astype(jnp.bfloat16)
    contrib_im = jnp.imag(spectrum).astype(jnp.bfloat16)

    def assemble(pieces):
        layout = pieces.reshape(FGRID, FGRID, NPOL, MC, NSUB, MC)
        return jnp.transpose(layout, (4, 2, 0, 3, 1, 5)).reshape(NSUB, NPOL, SG, SG)
    table_re, table_im = dft_table(SG)
    phase_grid = chirp_phase(0, SG, SG)

    def one_subgrid(inputs):
        layout_re, layout_im, rows_u, rows_v, weights_w = inputs
        flat_u = rows_u.reshape(TMO * VT, SG)
        flat_v = rows_v.reshape(TMO * VT, SG)
        flat_w = jnp.transpose(weights_w, (1, 0, 2)).reshape(NW, TMO * VT)
        results = []
        for polarisation in range(NPOL):
            half_re = (real_dot(layout_re[polarisation], table_re) - real_dot(layout_im[polarisation], table_im)).astype(jnp.bfloat16)
            half_im = (real_dot(layout_re[polarisation], table_im) + real_dot(layout_im[polarisation], table_re)).astype(jnp.bfloat16)
            sub_real = (real_dot(table_re, half_re) - real_dot(table_im, half_im)).astype(jnp.bfloat16)
            sub_imag = (real_dot(table_re, half_im) + real_dot(table_im, half_re)).astype(jnp.bfloat16)
            layers = make_planes(sub_real, sub_imag, phase_grid, NW)
            results.append(degrid_reference(layers, flat_u, flat_v, flat_w))
        return jnp.stack(results).reshape(NPOL, 2, TMO, VT)
    predicted = lax.map(one_subgrid, (assemble(contrib_re), assemble(contrib_im), taper_leading_axis, taper_trailing_axis, depth_layer_factors))
    slot_index = jnp.arange(VT, dtype=jnp.int32)
    slot_live, channel, antenna_couple = decode_slots(visibility_groups_table, slot_index)
    antenna_left = jnp.take(antenna_links[0], antenna_couple)
    antenna_right = jnp.take(antenna_links[1], antenna_couple)
    gains_turned = jnp.transpose(complex_receiver_factors, (0, 2, 1))
    gain_first = gains_turned[channel, antenna_left]
    gain_second = gains_turned[channel, antenna_right]
    pred_re = jnp.transpose(predicted[:, :, 0], (0, 2, 3, 1))
    pred_im = jnp.transpose(predicted[:, :, 1], (0, 2, 3, 1))
    obs_re = jnp.transpose(measured_correlations[:, 0::2], (0, 2, 3, 1))
    obs_im = jnp.transpose(measured_correlations[:, 1::2], (0, 2, 3, 1))
    resid_re, resid_im, leading, trailing = model_terms(pred_re, pred_im, obs_re, obs_im, gain_first, gain_second, slot_live)
    residual = jnp.transpose(jnp.stack([resid_re, resid_im], axis=-1), (0, 3, 4, 1, 2)).reshape(NSUB, 2 * NPOL, TMO, VT)
    segments_first = (antenna_left * NCH + channel).reshape(-1).astype(jnp.int32)
    segments_second = (antenna_right * NCH + channel).reshape(-1).astype(jnp.int32)
    summed = jax.ops.segment_sum(leading.reshape(-1, 4), segments_first, num_segments=NST * NCH)
    summed = summed + jax.ops.segment_sum(trailing.reshape(-1, 4), segments_second, num_segments=NST * NCH)
    gain_grad = grad_scale * summed.reshape(NST, NCH * 4)
    return (residual, gain_grad)
```

```python
import functools
import math

import jax
import jax.numpy as jnp
import ml_dtypes
import numpy as np
from jax import lax
from jax.experimental import pallas as pl
from jax.experimental.pallas import tpu as pltpu
from jax.sharding import PartitionSpec as P

FGRID = 8
FS = 4096
MC = 64
SG = 512
NPOL = 4
NW = 2
NCH = 256
NST = 512
VT = 128
NBLK = 8
LINK_WINDOW = 256

w_chirp = 0.37
grad_scale = 0.1
MIB = 1 << 20

bf16 = jnp.bfloat16
f32 = jnp.float32
NT = (((1,), (1,)), ((), ()))


def dot_nt(left, right):
    return lax.dot_general(left, right, NT, preferred_element_type=f32)


def np_bf16(table):
    return np.asarray(table, np.float64).astype(np.float32).astype(ml_dtypes.bfloat16)


@functools.cache
def section_tables():
    a = np.arange(32)
    angle = -2 * np.pi * ((a[:, None] * a[None, :]) % 32) / 32
    c, s = np.cos(angle), np.sin(angle)
    first = np.block([[c, -s], [s, c]])
    k = np.arange(64)[:, None]
    l = np.arange(128)[None, :]
    turn = -2 * np.pi * ((k * l) % FS) / FS
    sub = np.arange(64)[:, None]
    angle = -2 * np.pi * ((sub * l) % 64) / 64
    last = np.concatenate([np.cos(angle), np.sin(angle)], axis=1) / math.sqrt(FS)
    return (
        np_bf16(first),
        np.stack([np.cos(turn), np.sin(turn)]).astype(np.float32),
        np_bf16(last),
    )


@functools.cache
def taper_tables():
    x = np.arange(SG)
    angle = 2 * np.pi * ((x[:, None] * x[None, :]) % SG) / SG
    table = np.exp(1j * angle) / math.sqrt(SG)
    across = (x - SG // 2) ** 2 * (w_chirp / SG**2)
    trailing, leading = [], []
    for w in range(NW):
        full = table * np.exp(2j * np.pi * w * across)[None, :]
        rows = np.stack([full.real, -full.imag]).reshape(2, FGRID, MC, SG)
        trailing.append(rows.transpose(1, 0, 2, 3).reshape(2 * SG, SG))
        halves = np.stack([full.real, full.imag]).reshape(2, FGRID, 2, MC // 2, SG)
        leading.append(halves.transpose(2, 0, 1, 3, 4).reshape(2, 2 * SG // 2, SG))
    return np_bf16(np.stack(trailing)), np_bf16(np.stack(leading, axis=1))


def contrib_kernel(x_ref, u_ref, v_ref, w_ref, first_ref, turn_ref, last_ref, out_ref, pack_ref, spread, lined, placed):
    rows = x_ref.shape[1]
    pack_ref[0:VT, :] = u_ref[...]
    pack_ref[VT : 2 * VT, :] = v_ref[...]
    pack_ref[2 * VT : 2 * VT + 16, :] = jnp.zeros((16, SG), bf16)
    pack_ref[2 * VT : 2 * VT + 16, 0:VT] = w_ref[...]
    for part in range(2):
        for a in range(32):
            at = (part * 32 + a) * rows
            spread[at : at + rows, :] = x_ref[part, :, a * 128 : (a + 1) * 128].astype(f32)
    for m in range(rows):
        lined[:, m * 128 : (m + 1) * 128] = spread[pl.ds(m, 64, stride=rows), :].astype(bf16)
    turn_re = turn_ref[0]
    turn_im = turn_ref[1]
    for pair in range(rows // 2):
        section = jnp.dot(
            first_ref[...], lined[:, pair * 256 : (pair + 1) * 256], preferred_element_type=f32
        )
        sides = []
        for half in range(2):
            one = section[:, half * 128 : (half + 1) * 128]
            re = jnp.concatenate([one[0:32], one[0:32]], axis=0)
            im = jnp.concatenate([one[32:64], one[32:64]], axis=0)
            turned_re = (re * turn_re - im * turn_im).astype(bf16)
            turned_im = (re * turn_im + im * turn_re).astype(bf16)
            sides.append(
                jnp.concatenate(
                    [
                        jnp.concatenate([turned_re, -turned_im], axis=1),
                        jnp.concatenate([turned_im, turned_re], axis=1),
                    ],
                    axis=0,
                )
            )
        result = dot_nt(last_ref[...], jnp.concatenate(sides, axis=0))
        placed[pl.ds(2 * pair, 64, stride=rows), :] = result[:, 0:128]
        placed[pl.ds(2 * pair + 1, 64, stride=rows), :] = result[:, 128:256]
    for s in range(64):
        out_ref[s] = placed[s * rows : (s + 1) * rows, :].astype(bf16)


def contributions(x, u, v, w):
    rows = x.shape[1]
    first, turn, last = section_tables()
    return pl.pallas_call(
        contrib_kernel,
        out_shape=(
            jax.ShapeDtypeStruct((64, rows, 128), bf16),
            jax.ShapeDtypeStruct((2 * VT + 16, SG), bf16),
        ),
        scratch_shapes=[
            pltpu.VMEM((64 * rows, 128), f32),
            pltpu.VMEM((64, 128 * rows), bf16),
            pltpu.VMEM((64 * rows, 128), f32),
        ],
        compiler_params=pltpu.CompilerParams(vmem_limit_bytes=16 * MIB),
        cost_estimate=pl.CostEstimate(flops=300_000_000, bytes_accessed=2 * MIB, transcendentals=0),
        name="contrib",
    )(x, u, v, w, jnp.asarray(first), jnp.asarray(turn), jnp.asarray(last))


def taper_kernel(sc_ref, u_ref, v_ref, w_ref, other_ref, trail_ref, lead_ref, b_ref, a_ref):
    del sc_ref
    v_all = jnp.concatenate([v_ref[...], other_ref[VT : 2 * VT, :]], axis=0)
    u_all = jnp.concatenate([u_ref[...], other_ref[0:VT, :]], axis=0)
    weights = jnp.concatenate([w_ref[...], other_ref[2 * VT : 2 * VT + 16, 0:VT]], axis=1).astype(f32)
    for w in range(NW):
        re_at = slice(w * 256, (w + 1) * 256)
        im_at = slice(512 + w * 256, 512 + (w + 1) * 256)
        for j in range(FGRID):
            got = dot_nt(trail_ref[w, j * 128 : (j + 1) * 128, :], v_all)
            b_ref[j * 128 : (j + 1) * 128, re_at] = got.astype(bf16)
            b_ref[j * 128 : j * 128 + 64, im_at] = (-got[64:128]).astype(bf16)
            b_ref[j * 128 + 64 : (j + 1) * 128, im_at] = got[0:64].astype(bf16)
        scale = weights[w : w + 1, :]
        a_ref[0, :, re_at] = dot_nt(lead_ref[w, 0:256, :], u_all) * scale
        a_ref[1, :, re_at] = dot_nt(lead_ref[w, 256:512, :], u_all) * scale


def taper_transforms(where, u, v, w, other):
    trailing, leading = taper_tables()
    whole = lambda shape: pl.BlockSpec(shape, lambda i, sc: (0,) * len(shape))
    return pl.pallas_call(
        taper_kernel,
        out_shape=(
            jax.ShapeDtypeStruct((2 * SG, 1024), bf16),
            jax.ShapeDtypeStruct((2, SG // 2, 512), f32),
        ),
        grid_spec=pltpu.PrefetchScalarGridSpec(
            num_scalar_prefetch=1,
            grid=(1,),
            in_specs=[
                whole((VT, SG)),
                whole((VT, SG)),
                whole((16, VT)),
                whole((2 * VT + 16, SG)),
                whole((NW, 2 * SG, SG)),
                pl.BlockSpec((None, NW, SG, SG), lambda i, sc: (sc[2], 0, 0, 0)),
            ],
            out_specs=(whole((2 * SG, 1024)), whole((2, SG // 2, 512))),
        ),
        compiler_params=pltpu.CompilerParams(vmem_limit_bytes=24 * MIB),
        cost_estimate=pl.CostEstimate(flops=800_000_000, bytes_accessed=8 * MIB, transcendentals=0),
        name="tapers",
    )(where, u, v, w, other, jnp.asarray(trailing), jnp.asarray(leading))


def slots_kernel(sc_ref, table_ref, obs_ref, links_ref, gains_ref, out_ref, window, factors, link_sem, gain_sem):
    tiles = links_ref.shape[1] // 128
    begin = jnp.int32(0)
    blocks = []
    copies = []
    for b in range(NBLK):
        channel = table_ref[0, b]
        offset = table_ref[1, b]
        amount = table_ref[2, b]
        tile = jnp.minimum(offset // 128, tiles - LINK_WINDOW // 128)
        at = pl.multiple_of(tile * 128, 128)
        copies.append(
            pltpu.make_async_copy(links_ref.at[:, pl.ds(at, LINK_WINDOW)], window.at[b], link_sem.at[b])
        )
        copies.append(pltpu.make_async_copy(gains_ref.at[channel], factors.at[b], gain_sem.at[b]))
        blocks.append((channel, offset - at, amount, begin))
        begin = begin + amount
    for copy in copies:
        copy.start()
    slot = lax.broadcasted_iota(jnp.int32, (1, VT), 1)
    members = []
    chooser = []
    live = jnp.zeros((1, VT), f32)
    channels = jnp.zeros((1, VT), f32)
    index = lax.broadcasted_iota(jnp.int32, (LINK_WINDOW, VT), 0)
    for channel, shift, amount, start in blocks:
        inside = (slot >= start) & (slot < start + amount)
        member = jnp.where(inside, 1.0, 0.0)
        members.append(member)
        live = live + member
        channels = channels + member * channel.astype(f32)
        want = jnp.where(inside, slot - start + shift, -1)
        chooser.append(jnp.where(index == want, 1.0, 0.0).astype(bf16))
    for copy in copies:
        copy.wait()
    digits = []
    for b in range(NBLK):
        found = window[b]
        high = found >> 4
        digits.append(jnp.concatenate([high, found - (high << 4)], axis=0).astype(f32).astype(bf16))
    picked = jnp.dot(
        jnp.concatenate(digits, axis=1), jnp.concatenate(chooser, axis=0), preferred_element_type=f32
    )
    stations = picked[0:2] * 16.0 + picked[2:4]
    both = jnp.concatenate([stations[0:1], stations[1:2]], axis=1).astype(jnp.int32)
    station_index = lax.broadcasted_iota(jnp.int32, (NST, 2 * VT), 0)
    onehot = jnp.where(station_index == both, 1.0, 0.0).astype(bf16)
    rest = jnp.concatenate([factors[b] for b in range(NBLK)], axis=0)
    taken = jnp.zeros((4 * NBLK, 2 * VT), f32)
    for piece in range(3):
        rounded = rest.astype(bf16)
        taken = taken + jnp.dot(rounded, onehot, preferred_element_type=f32)
        rest = rest - rounded.astype(f32)
    gain_first = jnp.zeros((4, VT), f32)
    gain_second = jnp.zeros((4, VT), f32)
    for b in range(NBLK):
        gain_first = gain_first + members[b] * taken[4 * b : 4 * b + 4, 0:VT]
        gain_second = gain_second + members[b] * taken[4 * b : 4 * b + 4, VT : 2 * VT]
    quarter = obs_ref.shape[3]
    lane = lax.broadcasted_iota(jnp.int32, (1, VT), 1)
    mine = (lane // quarter) == sc_ref[1]
    out_ref[0:4, :] = jnp.zeros((4, VT), f32)
    for row in range(2 * NPOL):
        one = obs_ref[0, row]
        spread = jnp.concatenate([one] * (VT // quarter), axis=1)
        out_ref[4 + row : 5 + row, :] = jnp.where(mine, spread, 0.0)
    out_ref[12:16, :] = gain_first
    out_ref[16:20, :] = gain_second
    out_ref[20:22, :] = stations
    out_ref[22:23, :] = channels
    out_ref[23:24, :] = live


def slot_rows(where, table, observed, links, gains):
    smem = pl.BlockSpec(memory_space=pltpu.SMEM)
    anywhere = pl.BlockSpec(memory_space=pl.ANY)
    return pl.pallas_call(
        slots_kernel,
        out_shape=jax.ShapeDtypeStruct((24, VT), f32),
        in_specs=[smem, smem, pl.BlockSpec(memory_space=pltpu.VMEM), anywhere, anywhere],
        out_specs=pl.BlockSpec(memory_space=pltpu.VMEM),
        scratch_shapes=[
            pltpu.VMEM((NBLK, 2, LINK_WINDOW), jnp.int32),
            pltpu.VMEM((NBLK, 4, NST), f32),
            pltpu.SemaphoreType.DMA((NBLK,)),
            pltpu.SemaphoreType.DMA((NBLK,)),
        ],
        compiler_params=pltpu.CompilerParams(vmem_limit_bytes=8 * MIB),
        cost_estimate=pl.CostEstimate(flops=50_000_000, bytes_accessed=2 * MIB, transcendentals=0),
        name="slots",
    )(where, table, observed, links, gains)


def predict_kernel(sc_ref, got_ref, b_ref, a_ref, info_ref, out_ref):
    rows = got_ref.shape[1]
    left = jnp.concatenate(
        [
            jnp.concatenate([got_ref[i * FGRID + j] for j in range(FGRID)], axis=1)
            for i in range(FGRID)
        ],
        axis=0,
    )
    del rows
    total_re = [jnp.zeros((1, VT), f32), jnp.zeros((1, VT), f32)]
    total_im = [jnp.zeros((1, VT), f32), jnp.zeros((1, VT), f32)]
    for w in range(NW):
        at = slice(w * 256, (w + 1) * 256)
        along_re = jnp.dot(left, b_ref[:, w * 256 : (w + 1) * 256], preferred_element_type=f32)
        along_im = jnp.dot(left, b_ref[:, 512 + w * 256 : 512 + (w + 1) * 256], preferred_element_type=f32)
        a_re = a_ref[0, :, at]
        a_im = a_ref[1, :, at]
        sum_re = jnp.sum(a_re * along_re - a_im * along_im, axis=0, keepdims=True)
        sum_im = jnp.sum(a_re * along_im + a_im * along_re, axis=0, keepdims=True)
        for side in range(2):
            total_re[side] = total_re[side] + sum_re[:, side * VT : (side + 1) * VT]
            total_im[side] = total_im[side] + sum_im[:, side * VT : (side + 1) * VT]
    first = sc_ref[2] == 0
    rows_out = [
        jnp.where(first, total_re[0], total_re[1]),
        jnp.where(first, total_re[1], total_re[0]),
        jnp.where(first, total_im[0], total_im[1]),
        jnp.where(first, total_im[1], total_im[0]),
    ]
    head = jnp.concatenate(rows_out + [info_ref[4:8, :]], axis=0)
    for to in range(out_ref.shape[0]):
        out_ref[to, 0:8, :] = head
        out_ref[to, 8:24, :] = info_ref[8:24, :]


def partial_predictions(where, got, b, a, info, peers):
    vmem = pl.BlockSpec(memory_space=pltpu.VMEM)
    return pl.pallas_call(
        predict_kernel,
        out_shape=jax.ShapeDtypeStruct((peers, 24, VT), f32),
        in_specs=[pl.BlockSpec(memory_space=pltpu.SMEM), vmem, vmem, vmem, vmem],
        out_specs=vmem,
        compiler_params=pltpu.CompilerParams(vmem_limit_bytes=20 * MIB),
        cost_estimate=pl.CostEstimate(flops=540_000_000, bytes_accessed=4 * MIB, transcendentals=0),
        name="predict",
    )(where, got, b, a, info)


def gradient_kernel(sc_ref, got_ref, resid_ref, out_ref):
    owners = 2
    own_class = sc_ref[1] * owners + sc_ref[2]
    row_id = lax.broadcasted_iota(jnp.int32, (SG, VT), 0)
    lane_of = lax.broadcasted_iota(jnp.int32, (VT, VT), 0)
    pick = lambda rows, order: jnp.concatenate([rows[i : i + 1] for i in order], axis=0)
    masks = {}
    values = {}
    resid_owner = []
    for o in range(owners):
        info = got_ref[o]
        measured = got_ref[o, 4:12, :]
        for p in range(1, NPOL):
            measured = measured + got_ref[p * owners + o, 4:12, :]
        pred_re = []
        pred_im = []
        for p in range(NPOL):
            one, two = got_ref[p * owners], got_ref[p * owners + 1]
            pred_re.append(one[o : o + 1] + two[o : o + 1])
            pred_im.append(one[2 + o : 3 + o] + two[2 + o : 3 + o])
        pred_re = jnp.concatenate(pred_re, axis=0)
        pred_im = jnp.concatenate(pred_im, axis=0)
        gain_first = info[12:16]
        gain_second = info[16:20]
        live = info[23:24]
        first_re = pick(gain_first, (0, 0, 2, 2))
        first_im = pick(gain_first, (1, 1, 3, 3))
        second_re = pick(gain_second, (0, 2, 0, 2))
        second_im = pick(gain_second, (1, 3, 1, 3))
        obs_re = pick(measured, (0, 2, 4, 6))
        obs_im = pick(measured, (1, 3, 5, 7))
        both_re = first_re * second_re + first_im * second_im
        both_im = first_im * second_re - first_re * second_im
        resid_re = live * (obs_re - (both_re * pred_re - both_im * pred_im))
        resid_im = live * (obs_im - (both_re * pred_im + both_im * pred_re))
        cross_re = second_re * pred_re + second_im * pred_im
        cross_im = second_im * pred_re - second_re * pred_im
        lead_re = -(resid_re * cross_re - resid_im * cross_im)
        lead_im = -(resid_re * cross_im + resid_im * cross_re)
        along_re = first_re * pred_re - first_im * pred_im
        along_im = first_re * pred_im + first_im * pred_re
        trail_re = -(resid_re * along_re + resid_im * along_im)
        trail_im = -(resid_re * along_im - resid_im * along_re)
        leading = jnp.concatenate(
            [
                lead_re[0:1] + lead_re[1:2],
                lead_im[0:1] + lead_im[1:2],
                lead_re[2:3] + lead_re[3:4],
                lead_im[2:3] + lead_im[3:4],
            ],
            axis=0,
        )
        trailing = jnp.concatenate(
            [
                trail_re[0:1] + trail_re[2:3],
                trail_im[0:1] + trail_im[2:3],
                trail_re[1:2] + trail_re[3:4],
                trail_im[1:2] + trail_im[3:4],
            ],
            axis=0,
        )
        resid_owner.append(
            jnp.concatenate(
                [r for p in range(NPOL) for r in (resid_re[p : p + 1], resid_im[p : p + 1])], axis=0
            )
        )
        channel = info[22:23].astype(jnp.int32)
        chosen = (lane_of >> 2) == (channel & 31)
        for side, terms in ((0, leading), (1, trailing)):
            station = info[20 + side : 21 + side].astype(jnp.int32)
            key = jnp.where((station & 7) == own_class, (station >> 3) * 8 + (channel >> 5), -1)
            masks[side, o] = jnp.where(row_id == key, 1.0, 0.0).astype(bf16)
            tall = jnp.concatenate([terms, terms], axis=0)
            tall = jnp.concatenate([tall] * 16, axis=0)
            values[side, o] = jnp.where(chosen, tall, 0.0).astype(bf16)
    order = [(side, o) for side in range(2) for o in range(owners)]
    mask = jnp.concatenate([masks[at] for at in order], axis=1)
    value = jnp.concatenate([values[at] for at in order], axis=1)
    out_ref[...] = dot_nt(mask, value).astype(bf16)
    mine = jnp.where(sc_ref[2] == 0, resid_owner[0], resid_owner[1])
    quarter = resid_ref.shape[3]
    part = mine[:, 0:quarter]
    for q in range(1, NPOL):
        part = jnp.where(sc_ref[1] == q, mine[:, q * quarter : (q + 1) * quarter], part)
    for row in range(2 * NPOL):
        resid_ref[0, row] = part[row : row + 1, :]


def gradient_rows(where, got, quarter):
    vmem = pl.BlockSpec(memory_space=pltpu.VMEM)
    return pl.pallas_call(
        gradient_kernel,
        out_shape=(
            jax.ShapeDtypeStruct((1, 2 * NPOL, 1, quarter), f32),
            jax.ShapeDtypeStruct((SG, 128), bf16),
        ),
        in_specs=[pl.BlockSpec(memory_space=pltpu.SMEM), vmem],
        out_specs=(vmem, vmem),
        compiler_params=pltpu.CompilerParams(vmem_limit_bytes=12 * MIB),
        cost_estimate=pl.CostEstimate(flops=70_000_000, bytes_accessed=MIB, transcendentals=0),
        name="gradient",
    )(where, got)


def on_device(
    tile_spectral_lines,
    taper_leading_axis,
    taper_trailing_axis,
    depth_layer_factors,
    measured_correlations,
    visibility_groups_table,
    antenna_links,
    complex_receiver_factors,
):
    where = jnp.stack([lax.axis_index("facet"), lax.axis_index("pol"), lax.axis_index("tm")]).astype(jnp.int32)
    quarter = measured_correlations.shape[3]
    u = taper_leading_axis.reshape(VT, SG)
    v = taper_trailing_axis.reshape(VT, SG)
    w = jnp.pad(depth_layer_factors.reshape(NW, VT), ((0, 16 - NW), (0, 0)))
    x = tile_spectral_lines.reshape(tile_spectral_lines.shape[2:])
    contrib, pack = contributions(x, u, v, w)
    received = lax.all_to_all(contrib, "facet", split_axis=0, concat_axis=0, tiled=True)
    other = lax.ppermute(pack, "tm", [(0, 1), (1, 0)])
    b, a = taper_transforms(where, u, v, w, other)
    info = slot_rows(
        where,
        visibility_groups_table.reshape(3, NBLK),
        measured_correlations,
        antenna_links,
        complex_receiver_factors,
    )
    peers = lax.axis_size(("pol", "tm"))
    sent = partial_predictions(where, received, b, a, info, peers)
    gathered = lax.all_to_all(sent, ("pol", "tm"), split_axis=0, concat_axis=0, tiled=True)
    residual, partial_rows = gradient_rows(where, gathered, quarter)
    rows = lax.all_to_all(
        partial_rows.reshape(64, 8, 128), "facet", split_axis=0, concat_axis=0, tiled=True
    )
    gain_grad = grad_scale * jnp.sum(rows.astype(f32), axis=0)
    return (residual, gain_grad.reshape(1, 4 * NCH))


def solution(mesh):
    return jax.shard_map(
        on_device,
        mesh=mesh,
        in_specs=(
            P("facet", "pol", None, "tm", None),
            P("facet", "tm", None, None),
            P("facet", "tm", None, None),
            P("facet", "tm", None, None),
            P("facet", None, "tm", "pol"),
            P("facet", "tm", None, None),
            P(),
            P(),
        ),
        out_specs=(P("facet", None, "tm", "pol"), P(("facet", "pol", "tm"), None)),
        check_vma=False,
    )
```

```python
import functools
import math

import jax
import jax.numpy as jnp
import ml_dtypes
import numpy as np
from jax import lax
from jax.experimental import pallas as pl
from jax.experimental.pallas import tpu as pltpu
from jax.sharding import PartitionSpec as P

FGRID = 8
FS = 4096
MC = 64
SG = 512
NPOL = 4
NW = 2
NCH = 256
NST = 512
VT = 128
NBLK = 8
LINK_WINDOW = 256
X_PIECES = 4

w_chirp = 0.37
grad_scale = 0.1
MIB = 1 << 20

bf16 = jnp.bfloat16
f32 = jnp.float32
NT = (((1,), (1,)), ((), ()))


def dot_nt(left, right):
    return lax.dot_general(left, right, NT, preferred_element_type=f32)


def np_bf16(table):
    return np.asarray(table, np.float64).astype(np.float32).astype(ml_dtypes.bfloat16)


@functools.cache
def section_tables():
    a = np.arange(32)
    angle = -2 * np.pi * ((a[:, None] * a[None, :]) % 32) / 32
    c, s = np.cos(angle), np.sin(angle)
    first = np.block([[c, -s], [s, c]])
    k = np.arange(64)[:, None]
    l = np.arange(128)[None, :]
    turn = -2 * np.pi * ((k * l) % FS) / FS
    sub = np.arange(64)[:, None]
    angle = -2 * np.pi * ((sub * l) % 64) / 64
    last = np.concatenate([np.cos(angle), np.sin(angle)], axis=1) / math.sqrt(FS)
    return (
        np_bf16(first),
        np.stack([np.cos(turn), np.sin(turn)]).astype(np.float32),
        np_bf16(last),
    )


@functools.cache
def taper_tables():
    x = np.arange(SG)
    angle = 2 * np.pi * ((x[:, None] * x[None, :]) % SG) / SG
    table = np.exp(1j * angle) / math.sqrt(SG)
    across = (x - SG // 2) ** 2 * (w_chirp / SG**2)
    trailing, leading = [], []
    for w in range(NW):
        full = table * np.exp(2j * np.pi * w * across)[None, :]
        rows = np.stack([full.real, -full.imag]).reshape(2, FGRID, MC, SG)
        trailing.append(rows.transpose(1, 0, 2, 3).reshape(2 * SG, SG))
        halves = np.stack([full.real, full.imag]).reshape(2, FGRID, 2, MC // 2, SG)
        leading.append(halves.transpose(2, 0, 1, 3, 4).reshape(2, 2 * SG // 2, SG))
    return np_bf16(np.stack(trailing)), np_bf16(np.stack(leading, axis=1))


def in_hbm(*arrays):
    return [pltpu.with_memory_space_constraint(one, pltpu.HBM) for one in arrays]


def contrib_kernel(
    x_hbm, u_hbm, v_hbm, w_hbm, first_hbm, turn_hbm, last_hbm,
    out_ref, pack_ref,
    x_ref, w_ref, first_ref, turn_ref, last_ref, spread, lined, placed, x_sem, sem,
):
    rows = x_ref.shape[1]
    chunk = FS // X_PIECES
    pieces = [
        pltpu.make_async_copy(
            x_hbm.at[:, :, pl.ds(c * chunk, chunk)], x_ref.at[:, :, pl.ds(c * chunk, chunk)], x_sem.at[c]
        )
        for c in range(X_PIECES)
    ]
    others = [
        pltpu.make_async_copy(source, target, sem.at[i])
        for i, (source, target) in enumerate(
            (
                (first_hbm, first_ref),
                (turn_hbm, turn_ref),
                (last_hbm, last_ref),
                (u_hbm, pack_ref.at[pl.ds(0, VT), :]),
                (v_hbm, pack_ref.at[pl.ds(VT, VT), :]),
                (w_hbm, w_ref),
            )
        )
    ]
    for copy in pieces + others:
        copy.start()
    per_piece = 32 // X_PIECES
    for c in range(X_PIECES):
        pieces[c].wait()
        for part in range(2):
            for a in range(c * per_piece, (c + 1) * per_piece):
                at = (part * 32 + a) * rows
                spread[at : at + rows, :] = x_ref[part, :, a * 128 : (a + 1) * 128].astype(f32)
    for copy in others:
        copy.wait()
    weights = jnp.concatenate([w_ref[...].astype(f32), jnp.zeros((16 - NW, VT), f32)], axis=0).astype(bf16)
    pack_ref[2 * VT : 2 * VT + 16, :] = jnp.concatenate([weights] * (SG // VT), axis=1)
    for m in range(rows):
        lined[:, m * 128 : (m + 1) * 128] = spread[pl.ds(m, 64, stride=rows), :].astype(bf16)
    turn_re = turn_ref[0]
    turn_im = turn_ref[1]
    for pair in range(rows // 2):
        section = jnp.dot(
            first_ref[...], lined[:, pair * 256 : (pair + 1) * 256], preferred_element_type=f32
        )
        sides = []
        for half in range(2):
            one = section[:, half * 128 : (half + 1) * 128]
            re = jnp.concatenate([one[0:32], one[0:32]], axis=0)
            im = jnp.concatenate([one[32:64], one[32:64]], axis=0)
            turned_re = (re * turn_re - im * turn_im).astype(bf16)
            turned_im = (re * turn_im + im * turn_re).astype(bf16)
            sides.append(
                jnp.concatenate(
                    [
                        jnp.concatenate([turned_re, -turned_im], axis=1),
                        jnp.concatenate([turned_im, turned_re], axis=1),
                    ],
                    axis=0,
                )
            )
        result = dot_nt(last_ref[...], jnp.concatenate(sides, axis=0))
        placed[pl.ds(2 * pair, 64, stride=rows), :] = result[:, 0:128]
        placed[pl.ds(2 * pair + 1, 64, stride=rows), :] = result[:, 128:256]
    for s in range(64):
        out_ref[s] = placed[s * rows : (s + 1) * rows, :].astype(bf16)


def contributions(x, u, v, w):
    rows = x.shape[1]
    first, turn, last = section_tables()
    anywhere = pl.BlockSpec(memory_space=pl.ANY)
    vmem = pl.BlockSpec(memory_space=pltpu.VMEM)
    return pl.pallas_call(
        contrib_kernel,
        out_shape=(
            pltpu.VMEM((64, rows, 128), bf16),
            pltpu.VMEM((2 * VT + 16, SG), bf16),
        ),
        in_specs=[anywhere] * 7,
        out_specs=(vmem, vmem),
        scratch_shapes=[
            pltpu.VMEM((2, rows, FS), bf16),
            pltpu.VMEM((NW, VT), bf16),
            pltpu.VMEM((64, 64), bf16),
            pltpu.VMEM((2, 64, 128), f32),
            pltpu.VMEM((64, 256), bf16),
            pltpu.VMEM((64 * rows, 128), f32),
            pltpu.VMEM((64, 128 * rows), bf16),
            pltpu.VMEM((64 * rows, 128), f32),
            pltpu.SemaphoreType.DMA((X_PIECES,)),
            pltpu.SemaphoreType.DMA((6,)),
        ],
        compiler_params=pltpu.CompilerParams(vmem_limit_bytes=16 * MIB),
        cost_estimate=pl.CostEstimate(flops=300_000_000, bytes_accessed=2 * MIB, transcendentals=0),
        name="contrib",
    )(*in_hbm(x, u, v, w, jnp.asarray(first), jnp.asarray(turn), jnp.asarray(last)))


def taper_kernel(sc_ref, own_ref, other_ref, trail_hbm, lead_hbm, b_ref, a_ref, trail_ref, lead_ref, sem):
    trail_copies = [
        pltpu.make_async_copy(trail_hbm.at[w], trail_ref.at[w], sem.at[w]) for w in range(NW)
    ]
    lead_copies = [
        pltpu.make_async_copy(lead_hbm.at[sc_ref[2], w], lead_ref.at[w], sem.at[NW + w]) for w in range(NW)
    ]
    for copy in trail_copies + lead_copies:
        copy.start()
    v_all = jnp.concatenate([own_ref[VT : 2 * VT, :], other_ref[VT : 2 * VT, :]], axis=0)
    u_all = jnp.concatenate([own_ref[0:VT, :], other_ref[0:VT, :]], axis=0)
    weights = jnp.concatenate(
        [own_ref[2 * VT : 2 * VT + 16, 0:VT], other_ref[2 * VT : 2 * VT + 16, 0:VT]], axis=1
    ).astype(f32)
    for w in range(NW):
        trail_copies[w].wait()
        re_at = slice(w * 256, (w + 1) * 256)
        im_at = slice(512 + w * 256, 512 + (w + 1) * 256)
        for j in range(FGRID):
            got = dot_nt(trail_ref[w, j * 128 : (j + 1) * 128, :], v_all)
            b_ref[j * 128 : (j + 1) * 128, re_at] = got.astype(bf16)
            b_ref[j * 128 : j * 128 + 64, im_at] = (-got[64:128]).astype(bf16)
            b_ref[j * 128 + 64 : (j + 1) * 128, im_at] = got[0:64].astype(bf16)
    for w in range(NW):
        lead_copies[w].wait()
        re_at = slice(w * 256, (w + 1) * 256)
        scale = weights[w : w + 1, :]
        a_ref[0, :, re_at] = (dot_nt(lead_ref[w, 0:256, :], u_all) * scale).astype(bf16)
        a_ref[1, :, re_at] = (dot_nt(lead_ref[w, 256:512, :], u_all) * scale).astype(bf16)


def taper_transforms(where, own, other):
    trailing, leading = taper_tables()
    anywhere = pl.BlockSpec(memory_space=pl.ANY)
    vmem = pl.BlockSpec(memory_space=pltpu.VMEM)
    return pl.pallas_call(
        taper_kernel,
        out_shape=(
            pltpu.VMEM((2 * SG, 1024), bf16),
            pltpu.VMEM((2, SG // 2, 512), bf16),
        ),
        in_specs=[pl.BlockSpec(memory_space=pltpu.SMEM), vmem, vmem, anywhere, anywhere],
        out_specs=(vmem, vmem),
        scratch_shapes=[
            pltpu.VMEM((NW, 2 * SG, SG), bf16),
            pltpu.VMEM((NW, SG, SG), bf16),
            pltpu.SemaphoreType.DMA((2 * NW,)),
        ],
        compiler_params=pltpu.CompilerParams(vmem_limit_bytes=24 * MIB),
        cost_estimate=pl.CostEstimate(flops=800_000_000, bytes_accessed=8 * MIB, transcendentals=0),
        name="tapers",
    )(where, own, other, *in_hbm(jnp.asarray(trailing), jnp.asarray(leading)))


def slots_kernel(sc_ref, table_ref, obs_ref, links_ref, gains_ref, out_ref, window, factors, link_sem, gain_sem):
    tiles = links_ref.shape[1] // 128
    begin = jnp.int32(0)
    blocks = []
    copies = []
    for b in range(NBLK):
        channel = table_ref[0, b]
        offset = table_ref[1, b]
        amount = table_ref[2, b]
        tile = jnp.minimum(offset // 128, tiles - LINK_WINDOW // 128)
        at = pl.multiple_of(tile * 128, 128)
        copies.append(
            pltpu.make_async_copy(links_ref.at[:, pl.ds(at, LINK_WINDOW)], window.at[b], link_sem.at[b])
        )
        copies.append(pltpu.make_async_copy(gains_ref.at[channel], factors.at[b], gain_sem.at[b]))
        blocks.append((channel, offset - at, amount, begin))
        begin = begin + amount
    for copy in copies:
        copy.start()
    slot = lax.broadcasted_iota(jnp.int32, (1, VT), 1)
    members = []
    chooser = []
    blocks_of = jnp.full((1, VT), -1.0, f32)
    channels = jnp.zeros((1, VT), f32)
    index = lax.broadcasted_iota(jnp.int32, (LINK_WINDOW, VT), 0)
    for b, (channel, shift, amount, start) in enumerate(blocks):
        inside = (slot >= start) & (slot < start + amount)
        member = jnp.where(inside, 1.0, 0.0)
        members.append(member)
        blocks_of = jnp.where(inside, float(b), blocks_of)
        channels = jnp.where(slot == NBLK * sc_ref[2] + (64 + b), channel.astype(f32), channels)
        want = jnp.where(inside, slot - start + shift, -1)
        chooser.append(jnp.where(index == want, 1.0, 0.0).astype(bf16))
    for copy in copies:
        copy.wait()
    digits = []
    for b in range(NBLK):
        found = window[b]
        high = found >> 4
        digits.append(jnp.concatenate([high, found - (high << 4)], axis=0).astype(f32).astype(bf16))
    picked = jnp.dot(
        jnp.concatenate(digits, axis=1), jnp.concatenate(chooser, axis=0), preferred_element_type=f32
    )
    stations = picked[0:2] * 16.0 + picked[2:4]
    both = jnp.concatenate([stations[0:1], stations[1:2]], axis=1).astype(jnp.int32)
    station_index = lax.broadcasted_iota(jnp.int32, (NST, 2 * VT), 0)
    onehot = jnp.where(station_index == both, 1.0, 0.0).astype(bf16)
    rest = jnp.concatenate([factors[b] for b in range(NBLK)], axis=0)
    taken = jnp.zeros((4 * NBLK, 2 * VT), f32)
    for piece in range(3):
        rounded = rest.astype(bf16)
        taken = taken + jnp.dot(rounded, onehot, preferred_element_type=f32)
        rest = rest - rounded.astype(f32)
    gain_first = jnp.zeros((4, VT), f32)
    gain_second = jnp.zeros((4, VT), f32)
    for b in range(NBLK):
        gain_first = gain_first + members[b] * taken[4 * b : 4 * b + 4, 0:VT]
        gain_second = gain_second + members[b] * taken[4 * b : 4 * b + 4, VT : 2 * VT]
    quarter = obs_ref.shape[3]
    lane = lax.broadcasted_iota(jnp.int32, (1, VT), 1)
    mine = (lane // quarter) == sc_ref[1]
    out_ref[0:4, :] = jnp.zeros((4, VT), f32)
    for row in range(2 * NPOL):
        one = obs_ref[0, row]
        spread = jnp.concatenate([one] * (VT // quarter), axis=1)
        out_ref[4 + row : 5 + row, :] = jnp.where(mine, spread, 0.0)
    out_ref[12:16, :] = gain_first
    out_ref[16:20, :] = gain_second
    out_ref[20:22, :] = stations
    out_ref[22:23, :] = blocks_of
    out_ref[23:24, :] = channels


def slot_rows(where, table, observed, links, gains):
    smem = pl.BlockSpec(memory_space=pltpu.SMEM)
    anywhere = pl.BlockSpec(memory_space=pl.ANY)
    return pl.pallas_call(
        slots_kernel,
        out_shape=jax.ShapeDtypeStruct((24, VT), f32),
        in_specs=[smem, smem, pl.BlockSpec(memory_space=pltpu.VMEM), anywhere, anywhere],
        out_specs=pl.BlockSpec(memory_space=pltpu.VMEM),
        scratch_shapes=[
            pltpu.VMEM((NBLK, 2, LINK_WINDOW), jnp.int32),
            pltpu.VMEM((NBLK, 4, NST), f32),
            pltpu.SemaphoreType.DMA((NBLK,)),
            pltpu.SemaphoreType.DMA((NBLK,)),
        ],
        compiler_params=pltpu.CompilerParams(vmem_limit_bytes=8 * MIB),
        cost_estimate=pl.CostEstimate(flops=50_000_000, bytes_accessed=2 * MIB, transcendentals=0),
        name="slots",
    )(where, table, observed, *in_hbm(links, gains))


def predict_kernel(sc_ref, got_ref, b_ref, a_ref, info_ref, out_ref):
    rows = got_ref.shape[1]
    left = jnp.concatenate(
        [
            jnp.concatenate([got_ref[i * FGRID + j] for j in range(FGRID)], axis=1)
            for i in range(FGRID)
        ],
        axis=0,
    )
    del rows
    total_re = [jnp.zeros((1, VT), f32), jnp.zeros((1, VT), f32)]
    total_im = [jnp.zeros((1, VT), f32), jnp.zeros((1, VT), f32)]
    for w in range(NW):
        at = slice(w * 256, (w + 1) * 256)
        along_re = jnp.dot(left, b_ref[:, w * 256 : (w + 1) * 256], preferred_element_type=f32)
        along_im = jnp.dot(left, b_ref[:, 512 + w * 256 : 512 + (w + 1) * 256], preferred_element_type=f32)
        a_re = a_ref[0, :, at].astype(f32)
        a_im = a_ref[1, :, at].astype(f32)
        sum_re = jnp.sum(a_re * along_re - a_im * along_im, axis=0, keepdims=True)
        sum_im = jnp.sum(a_re * along_im + a_im * along_re, axis=0, keepdims=True)
        for side in range(2):
            total_re[side] = total_re[side] + sum_re[:, side * VT : (side + 1) * VT]
            total_im[side] = total_im[side] + sum_im[:, side * VT : (side + 1) * VT]
    first = sc_ref[2] == 0
    rows_out = [
        jnp.where(first, total_re[0], total_re[1]),
        jnp.where(first, total_re[1], total_re[0]),
        jnp.where(first, total_im[0], total_im[1]),
        jnp.where(first, total_im[1], total_im[0]),
    ]
    head = jnp.concatenate(rows_out + [info_ref[4:8, :]], axis=0)
    for to in range(out_ref.shape[0]):
        out_ref[to, 0:8, :] = head
        out_ref[to, 8:24, :] = info_ref[8:24, :]


def partial_predictions(where, got, b, a, info, peers):
    vmem = pl.BlockSpec(memory_space=pltpu.VMEM)
    return pl.pallas_call(
        predict_kernel,
        out_shape=jax.ShapeDtypeStruct((peers, 24, VT), f32),
        in_specs=[pl.BlockSpec(memory_space=pltpu.SMEM), vmem, vmem, vmem, vmem],
        out_specs=vmem,
        compiler_params=pltpu.CompilerParams(vmem_limit_bytes=20 * MIB),
        cost_estimate=pl.CostEstimate(flops=540_000_000, bytes_accessed=4 * MIB, transcendentals=0),
        name="predict",
    )(where, got, b, a, info)


def gradient_kernel(sc_ref, got_ref, resid_ref, out_ref):
    owners = 2
    own_class = sc_ref[1] * owners + sc_ref[2]
    row_id = lax.broadcasted_iota(jnp.int32, (NST // 8, VT), 0)
    block_row = lax.broadcasted_iota(jnp.int32, (VT, VT), 0) >> 2
    channels = got_ref[0, 23:24, :] + got_ref[1, 23:24, :]
    pick = lambda rows, order: jnp.concatenate([rows[i : i + 1] for i in order], axis=0)
    masks = {}
    values = {}
    resid_owner = []
    for o in range(owners):
        info = got_ref[o]
        measured = got_ref[o, 4:12, :]
        for p in range(1, NPOL):
            measured = measured + got_ref[p * owners + o, 4:12, :]
        pred_re = []
        pred_im = []
        for p in range(NPOL):
            one, two = got_ref[p * owners], got_ref[p * owners + 1]
            pred_re.append(one[o : o + 1] + two[o : o + 1])
            pred_im.append(one[2 + o : 3 + o] + two[2 + o : 3 + o])
        pred_re = jnp.concatenate(pred_re, axis=0)
        pred_im = jnp.concatenate(pred_im, axis=0)
        gain_first = info[12:16]
        gain_second = info[16:20]
        block = info[22:23].astype(jnp.int32)
        live = jnp.where(block >= 0, 1.0, 0.0)
        first_re = pick(gain_first, (0, 0, 2, 2))
        first_im = pick(gain_first, (1, 1, 3, 3))
        second_re = pick(gain_second, (0, 2, 0, 2))
        second_im = pick(gain_second, (1, 3, 1, 3))
        obs_re = pick(measured, (0, 2, 4, 6))
        obs_im = pick(measured, (1, 3, 5, 7))
        both_re = first_re * second_re + first_im * second_im
        both_im = first_im * second_re - first_re * second_im
        resid_re = live * (obs_re - (both_re * pred_re - both_im * pred_im))
        resid_im = live * (obs_im - (both_re * pred_im + both_im * pred_re))
        cross_re = second_re * pred_re + second_im * pred_im
        cross_im = second_im * pred_re - second_re * pred_im
        lead_re = -(resid_re * cross_re - resid_im * cross_im)
        lead_im = -(resid_re * cross_im + resid_im * cross_re)
        along_re = first_re * pred_re - first_im * pred_im
        along_im = first_re * pred_im + first_im * pred_re
        trail_re = -(resid_re * along_re + resid_im * along_im)
        trail_im = -(resid_re * along_im - resid_im * along_re)
        leading = jnp.concatenate(
            [
                lead_re[0:1] + lead_re[1:2],
                lead_im[0:1] + lead_im[1:2],
                lead_re[2:3] + lead_re[3:4],
                lead_im[2:3] + lead_im[3:4],
            ],
            axis=0,
        )
        trailing = jnp.concatenate(
            [
                trail_re[0:1] + trail_re[2:3],
                trail_im[0:1] + trail_im[2:3],
                trail_re[1:2] + trail_re[3:4],
                trail_im[1:2] + trail_im[3:4],
            ],
            axis=0,
        )
        resid_owner.append(
            jnp.concatenate(
                [r for p in range(NPOL) for r in (resid_re[p : p + 1], resid_im[p : p + 1])], axis=0
            )
        )
        chosen = block_row == jnp.where(block >= 0, NBLK * o + block, -1)
        for side, terms in ((0, leading), (1, trailing)):
            station = info[20 + side : 21 + side].astype(jnp.int32)
            key = jnp.where((station & 7) == own_class, station >> 3, -1)
            masks[side, o] = jnp.where(row_id == key, 1.0, 0.0).astype(bf16)
            tall = jnp.concatenate([terms, terms], axis=0)
            tall = jnp.concatenate([tall] * 16, axis=0)
            values[side, o] = jnp.where(chosen, tall, 0.0).astype(bf16)
    order = [(side, o) for side in range(2) for o in range(owners)]
    mask = jnp.concatenate([masks[at] for at in order], axis=1)
    value = jnp.concatenate([values[at] for at in order], axis=1)
    out_ref[...] = dot_nt(mask, value) + channels
    mine = jnp.where(sc_ref[2] == 0, resid_owner[0], resid_owner[1])
    quarter = resid_ref.shape[3]
    part = mine[:, 0:quarter]
    for q in range(1, NPOL):
        part = jnp.where(sc_ref[1] == q, mine[:, q * quarter : (q + 1) * quarter], part)
    for row in range(2 * NPOL):
        resid_ref[0, row] = part[row : row + 1, :]


def gradient_rows(where, got, quarter):
    vmem = pl.BlockSpec(memory_space=pltpu.VMEM)
    return pl.pallas_call(
        gradient_kernel,
        out_shape=(
            jax.ShapeDtypeStruct((1, 2 * NPOL, 1, quarter), f32),
            jax.ShapeDtypeStruct((NST // 8, 128), f32),
        ),
        in_specs=[pl.BlockSpec(memory_space=pltpu.SMEM), vmem],
        out_specs=(vmem, vmem),
        compiler_params=pltpu.CompilerParams(vmem_limit_bytes=12 * MIB),
        cost_estimate=pl.CostEstimate(flops=70_000_000, bytes_accessed=MIB, transcendentals=0),
        name="gradient",
    )(where, got)


def collect_kernel(got_ref, out_ref):
    turned = got_ref[...].T
    lanes = turned.shape[1]
    channel_row = lax.broadcasted_iota(jnp.int32, (128, lanes), 0) >> 2
    group_row = lax.broadcasted_iota(jnp.int32, (8, lanes), 0)
    total = jnp.zeros((8, 128), f32)
    for block in range(2 * NBLK):
        channel = turned[64 + block : 65 + block].astype(jnp.int32)
        terms = turned[4 * block : 4 * block + 4]
        tall = jnp.concatenate([terms, terms], axis=0)
        tall = jnp.concatenate([tall] * 16, axis=0)
        value = jnp.where(channel_row == (channel & 31), tall, 0.0).astype(bf16)
        group = jnp.where(group_row == (channel >> 5), 1.0, 0.0).astype(bf16)
        total = total + dot_nt(group, value)
    out_ref[...] = grad_scale * total


def collect_rows(got):
    vmem = pl.BlockSpec(memory_space=pltpu.VMEM)
    return pl.pallas_call(
        collect_kernel,
        out_shape=jax.ShapeDtypeStruct((8, 128), f32),
        in_specs=[vmem],
        out_specs=vmem,
        compiler_params=pltpu.CompilerParams(vmem_limit_bytes=8 * MIB),
        cost_estimate=pl.CostEstimate(flops=2_000_000, bytes_accessed=65536, transcendentals=0),
        name="collect",
    )(got)


def on_device(
    tile_spectral_lines,
    taper_leading_axis,
    taper_trailing_axis,
    depth_layer_factors,
    measured_correlations,
    visibility_groups_table,
    antenna_links,
    complex_receiver_factors,
):
    where = jnp.stack([lax.axis_index("facet"), lax.axis_index("pol"), lax.axis_index("tm")]).astype(jnp.int32)
    quarter = measured_correlations.shape[3]
    u = taper_leading_axis.reshape(VT, SG)
    v = taper_trailing_axis.reshape(VT, SG)
    w = depth_layer_factors.reshape(NW, VT)
    x = tile_spectral_lines.reshape(tile_spectral_lines.shape[2:])
    contrib, pack = contributions(x, u, v, w)
    received = lax.all_to_all(contrib, "facet", split_axis=0, concat_axis=0, tiled=True)
    other = lax.ppermute(pack, "tm", [(0, 1), (1, 0)])
    b, a = taper_transforms(where, pack, other)
    info = slot_rows(
        where,
        visibility_groups_table.reshape(3, NBLK),
        measured_correlations,
        antenna_links,
        complex_receiver_factors,
    )
    peers = lax.axis_size(("pol", "tm"))
    sent = partial_predictions(where, received, b, a, info, peers)
    gathered = lax.all_to_all(sent, ("pol", "tm"), split_axis=0, concat_axis=0, tiled=True)
    residual, partial_rows = gradient_rows(where, gathered, quarter)
    rows = lax.all_to_all(
        partial_rows.reshape(NST // 8, 1, 128), "facet", split_axis=0, concat_axis=0, tiled=True
    )
    gain_grad = collect_rows(rows.reshape(NST // 8, 128))
    return (residual, gain_grad.reshape(1, 4 * NCH))


def solution(mesh):
    return jax.shard_map(
        on_device,
        mesh=mesh,
        in_specs=(
            P("facet", "pol", None, "tm", None),
            P("facet", "tm", None, None),
            P("facet", "tm", None, None),
            P("facet", "tm", None, None),
            P("facet", None, "tm", "pol"),
            P("facet", "tm", None, None),
            P(),
            P(),
        ),
        out_specs=(P("facet", None, "tm", "pol"), P(("facet", "pol", "tm"), None)),
        check_vma=False,
    )
```

```python
import functools
import math

import jax
import jax.numpy as jnp
import ml_dtypes
import numpy as np
from jax import lax
from jax.experimental import pallas as pl
from jax.experimental.pallas import tpu as pltpu
from jax.sharding import PartitionSpec as P

FGRID = 8
FS = 4096
MC = 64
SG = 512
NPOL = 4
NW = 2
NCH = 256
NST = 512
VT = 128
NBLK = 8
LINK_WINDOW = 256
BATCHES = 2

w_chirp = 0.37
grad_scale = 0.1
MIB = 1 << 20

bf16 = jnp.bfloat16
f32 = jnp.float32
NT = (((1,), (1,)), ((), ()))


def dot_nt(left, right):
    return lax.dot_general(left, right, NT, preferred_element_type=f32)


def np_bf16(table):
    return np.asarray(table, np.float64).astype(np.float32).astype(ml_dtypes.bfloat16)


@functools.cache
def section_tables():
    a = np.arange(32)
    angle = -2 * np.pi * ((a[:, None] * a[None, :]) % 32) / 32
    c, s = np.cos(angle), np.sin(angle)
    first = np.block([[c, -s], [s, c]])
    k = np.arange(64)[:, None]
    l = np.arange(128)[None, :]
    turn = -2 * np.pi * ((k * l) % FS) / FS
    sub = np.arange(64)[:, None]
    angle = -2 * np.pi * ((sub * l) % 64) / 64
    last = np.concatenate([np.cos(angle), np.sin(angle)], axis=1) / math.sqrt(FS)
    return (
        np_bf16(first),
        np.stack([np.cos(turn), np.sin(turn)]).astype(np.float32),
        np_bf16(last),
    )


@functools.cache
def taper_tables():
    x = np.arange(SG)
    angle = 2 * np.pi * ((x[:, None] * x[None, :]) % SG) / SG
    table = np.exp(1j * angle) / math.sqrt(SG)
    across = (x - SG // 2) ** 2 * (w_chirp / SG**2)
    trailing, leading = [], []
    for w in range(NW):
        full = table * np.exp(2j * np.pi * w * across)[None, :]
        rows = np.stack([full.real, -full.imag]).reshape(2, FGRID, MC, SG)
        trailing.append(rows.transpose(1, 0, 2, 3).reshape(2 * SG, SG))
        halves = np.stack([full.real, full.imag]).reshape(2, FGRID, 2, MC // 2, SG)
        leading.append(halves.transpose(2, 0, 1, 3, 4).reshape(2, 2 * SG // 2, SG))
    return np_bf16(np.stack(trailing)), np_bf16(np.stack(leading, axis=1))


def in_hbm(*arrays):
    return [pltpu.with_memory_space_constraint(one, pltpu.HBM) for one in arrays]


def contrib_kernel(
    x_hbm, u_hbm, v_hbm, w_hbm, first_hbm, turn_hbm, last_hbm,
    out_hbm, pack_ref,
    x_ref, w_ref, first_ref, turn_ref, last_ref, spread, lined, placed, out_ref, x_sem, sem, out_sem,
):
    rows = x_ref.shape[1]
    batch = rows // BATCHES
    pieces = [
        pltpu.make_async_copy(
            x_hbm.at[:, pl.ds(h * batch, batch), :], x_ref.at[:, pl.ds(h * batch, batch), :], x_sem.at[h]
        )
        for h in range(BATCHES)
    ]
    tables = [
        pltpu.make_async_copy(source, target, sem.at[i])
        for i, (source, target) in enumerate(
            ((first_hbm, first_ref), (turn_hbm, turn_ref), (last_hbm, last_ref))
        )
    ]
    tapers = [
        pltpu.make_async_copy(source, target, sem.at[3 + i])
        for i, (source, target) in enumerate(
            (
                (w_hbm, w_ref),
                (u_hbm, pack_ref.at[pl.ds(0, VT), :]),
                (v_hbm, pack_ref.at[pl.ds(VT, VT), :]),
            )
        )
    ]
    results = [
        pltpu.make_async_copy(out_ref.at[h], out_hbm.at[:, pl.ds(h * batch, batch), :], out_sem.at[h])
        for h in range(BATCHES)
    ]
    for copy in pieces[:1] + tables + pieces[1:] + tapers:
        copy.start()

    def section_of(pair):
        return jnp.dot(first_ref[...], lined[:, pair * 256 : (pair + 1) * 256], preferred_element_type=f32)

    def turned_of(section):
        turn_re = turn_ref[0]
        turn_im = turn_ref[1]
        sides = []
        for half in range(2):
            one = section[:, half * 128 : (half + 1) * 128]
            re = jnp.concatenate([one[0:32], one[0:32]], axis=0)
            im = jnp.concatenate([one[32:64], one[32:64]], axis=0)
            turned_re = (re * turn_re - im * turn_im).astype(bf16)
            turned_im = (re * turn_im + im * turn_re).astype(bf16)
            sides.append(
                jnp.concatenate(
                    [
                        jnp.concatenate([turned_re, -turned_im], axis=1),
                        jnp.concatenate([turned_im, turned_re], axis=1),
                    ],
                    axis=0,
                )
            )
        return jnp.concatenate(sides, axis=0)

    def finish(pair, turned):
        result = dot_nt(last_ref[...], turned)
        placed[pl.ds(2 * pair, 64, stride=rows), :] = result[:, 0:128]
        placed[pl.ds(2 * pair + 1, 64, stride=rows), :] = result[:, 128:256]

    def line_up(h):
        pieces[h].wait()
        for part in range(2):
            for a in range(32):
                at = (part * 32 + a) * rows + h * batch
                spread[at : at + batch, :] = x_ref[
                    part, h * batch : (h + 1) * batch, a * 128 : (a + 1) * 128
                ].astype(f32)
        for m in range(h * batch, (h + 1) * batch):
            lined[:, m * 128 : (m + 1) * 128] = spread[pl.ds(m, 64, stride=rows), :].astype(bf16)

    def send(h):
        for s in range(64):
            at = s * rows + h * batch
            out_ref[h, s] = placed[at : at + batch, :].astype(bf16)
        results[h].start()

    per = batch // 2
    line_up(0)
    for copy in tables:
        copy.wait()
    pairs = rows // 2
    sections = {0: section_of(0), 1: section_of(1)}
    turned = {}
    for step in range(pairs + 1):
        if step + 2 < pairs:
            if (step + 2) % per == 0:
                line_up((step + 2) // per)
            sections[step + 2] = section_of(step + 2)
        if step < pairs:
            turned[step] = turned_of(sections.pop(step))
        if step >= 1:
            finish(step - 1, turned.pop(step - 1))
            if step % per == 0:
                send(step // per - 1)
    for copy in tapers:
        copy.wait()
    weights = jnp.concatenate([w_ref[...].astype(f32), jnp.zeros((16 - NW, VT), f32)], axis=0).astype(bf16)
    pack_ref[2 * VT : 2 * VT + 16, :] = jnp.concatenate([weights] * (SG // VT), axis=1)
    for copy in results:
        copy.wait()


def contributions(x, u, v, w):
    rows = x.shape[1]
    first, turn, last = section_tables()
    anywhere = pl.BlockSpec(memory_space=pl.ANY)
    vmem = pl.BlockSpec(memory_space=pltpu.VMEM)
    return pl.pallas_call(
        contrib_kernel,
        out_shape=(
            jax.ShapeDtypeStruct((64, rows, 128), bf16),
            pltpu.VMEM((2 * VT + 16, SG), bf16),
        ),
        in_specs=[anywhere] * 7,
        out_specs=(anywhere, vmem),
        scratch_shapes=[
            pltpu.VMEM((2, rows, FS), bf16),
            pltpu.VMEM((NW, VT), bf16),
            pltpu.VMEM((64, 64), bf16),
            pltpu.VMEM((2, 64, 128), f32),
            pltpu.VMEM((64, 256), bf16),
            pltpu.VMEM((64 * rows, 128), f32),
            pltpu.VMEM((64, 128 * rows), bf16),
            pltpu.VMEM((64 * rows, 128), f32),
            pltpu.VMEM((BATCHES, 64, rows // BATCHES, 128), bf16),
            pltpu.SemaphoreType.DMA((BATCHES,)),
            pltpu.SemaphoreType.DMA((6,)),
            pltpu.SemaphoreType.DMA((BATCHES,)),
        ],
        compiler_params=pltpu.CompilerParams(vmem_limit_bytes=16 * MIB),
        cost_estimate=pl.CostEstimate(flops=300_000_000, bytes_accessed=2 * MIB, transcendentals=0),
        name="contrib",
    )(*in_hbm(x, u, v, w, jnp.asarray(first), jnp.asarray(turn), jnp.asarray(last)))


def taper_kernel(sc_ref, own_ref, other_ref, trail_hbm, lead_hbm, b_ref, a_ref, trail_ref, lead_ref, sem):
    trail_copies = [
        pltpu.make_async_copy(trail_hbm.at[w], trail_ref.at[w], sem.at[w]) for w in range(NW)
    ]
    lead_copies = [
        pltpu.make_async_copy(lead_hbm.at[sc_ref[2], w], lead_ref.at[w], sem.at[NW + w]) for w in range(NW)
    ]
    for copy in trail_copies + lead_copies:
        copy.start()
    v_all = jnp.concatenate([own_ref[VT : 2 * VT, :], other_ref[VT : 2 * VT, :]], axis=0)
    u_all = jnp.concatenate([own_ref[0:VT, :], other_ref[0:VT, :]], axis=0)
    weights = jnp.concatenate(
        [own_ref[2 * VT : 2 * VT + 16, 0:VT], other_ref[2 * VT : 2 * VT + 16, 0:VT]], axis=1
    ).astype(f32)
    for w in range(NW):
        trail_copies[w].wait()
        re_at = slice(w * 256, (w + 1) * 256)
        im_at = slice(512 + w * 256, 512 + (w + 1) * 256)
        for j in range(FGRID):
            got = dot_nt(trail_ref[w, j * 128 : (j + 1) * 128, :], v_all)
            b_ref[j * 128 : (j + 1) * 128, re_at] = got.astype(bf16)
            b_ref[j * 128 : j * 128 + 64, im_at] = (-got[64:128]).astype(bf16)
            b_ref[j * 128 + 64 : (j + 1) * 128, im_at] = got[0:64].astype(bf16)
    for w in range(NW):
        lead_copies[w].wait()
        re_at = slice(w * 256, (w + 1) * 256)
        scale = weights[w : w + 1, :]
        a_ref[0, :, re_at] = (dot_nt(lead_ref[w, 0:256, :], u_all) * scale).astype(bf16)
        a_ref[1, :, re_at] = (dot_nt(lead_ref[w, 256:512, :], u_all) * scale).astype(bf16)


def taper_transforms(where, own, other):
    trailing, leading = taper_tables()
    anywhere = pl.BlockSpec(memory_space=pl.ANY)
    vmem = pl.BlockSpec(memory_space=pltpu.VMEM)
    return pl.pallas_call(
        taper_kernel,
        out_shape=(
            pltpu.VMEM((2 * SG, 1024), bf16),
            pltpu.VMEM((2, SG // 2, 512), bf16),
        ),
        in_specs=[pl.BlockSpec(memory_space=pltpu.SMEM), vmem, vmem, anywhere, anywhere],
        out_specs=(vmem, vmem),
        scratch_shapes=[
            pltpu.VMEM((NW, 2 * SG, SG), bf16),
            pltpu.VMEM((NW, SG, SG), bf16),
            pltpu.SemaphoreType.DMA((2 * NW,)),
        ],
        compiler_params=pltpu.CompilerParams(vmem_limit_bytes=24 * MIB),
        cost_estimate=pl.CostEstimate(flops=800_000_000, bytes_accessed=8 * MIB, transcendentals=0),
        name="tapers",
    )(where, own, other, *in_hbm(jnp.asarray(trailing), jnp.asarray(leading)))


def slots_kernel(sc_ref, table_ref, obs_ref, links_ref, gains_ref, out_ref, window, factors, link_sem, gain_sem):
    tiles = links_ref.shape[1] // 128
    begin = jnp.int32(0)
    blocks = []
    copies = []
    for b in range(NBLK):
        channel = table_ref[0, b]
        offset = table_ref[1, b]
        amount = table_ref[2, b]
        tile = jnp.minimum(offset // 128, tiles - LINK_WINDOW // 128)
        at = pl.multiple_of(tile * 128, 128)
        copies.append(
            pltpu.make_async_copy(links_ref.at[:, pl.ds(at, LINK_WINDOW)], window.at[b], link_sem.at[b])
        )
        copies.append(pltpu.make_async_copy(gains_ref.at[channel], factors.at[b], gain_sem.at[b]))
        blocks.append((channel, offset - at, amount, begin))
        begin = begin + amount
    for copy in copies:
        copy.start()
    slot = lax.broadcasted_iota(jnp.int32, (1, VT), 1)
    members = []
    chooser = []
    blocks_of = jnp.full((1, VT), -1.0, f32)
    channels = jnp.zeros((1, VT), f32)
    index = lax.broadcasted_iota(jnp.int32, (LINK_WINDOW, VT), 0)
    for b, (channel, shift, amount, start) in enumerate(blocks):
        inside = (slot >= start) & (slot < start + amount)
        member = jnp.where(inside, 1.0, 0.0)
        members.append(member)
        blocks_of = jnp.where(inside, float(b), blocks_of)
        channels = jnp.where(slot == NBLK * sc_ref[2] + (64 + b), channel.astype(f32), channels)
        want = jnp.where(inside, slot - start + shift, -1)
        chooser.append(jnp.where(index == want, 1.0, 0.0).astype(bf16))
    for copy in copies:
        copy.wait()
    digits = []
    for b in range(NBLK):
        found = window[b]
        high = found >> 4
        digits.append(jnp.concatenate([high, found - (high << 4)], axis=0).astype(f32).astype(bf16))
    picked = jnp.dot(
        jnp.concatenate(digits, axis=1), jnp.concatenate(chooser, axis=0), preferred_element_type=f32
    )
    stations = picked[0:2] * 16.0 + picked[2:4]
    both = jnp.concatenate([stations[0:1], stations[1:2]], axis=1).astype(jnp.int32)
    station_index = lax.broadcasted_iota(jnp.int32, (NST, 2 * VT), 0)
    onehot = jnp.where(station_index == both, 1.0, 0.0).astype(bf16)
    rest = jnp.concatenate([factors[b] for b in range(NBLK)], axis=0)
    taken = jnp.zeros((4 * NBLK, 2 * VT), f32)
    for piece in range(3):
        rounded = rest.astype(bf16)
        taken = taken + jnp.dot(rounded, onehot, preferred_element_type=f32)
        rest = rest - rounded.astype(f32)
    gain_first = jnp.zeros((4, VT), f32)
    gain_second = jnp.zeros((4, VT), f32)
    for b in range(NBLK):
        gain_first = gain_first + members[b] * taken[4 * b : 4 * b + 4, 0:VT]
        gain_second = gain_second + members[b] * taken[4 * b : 4 * b + 4, VT : 2 * VT]
    quarter = obs_ref.shape[3]
    lane = lax.broadcasted_iota(jnp.int32, (1, VT), 1)
    mine = (lane // quarter) == sc_ref[1]
    out_ref[0:4, :] = jnp.zeros((4, VT), f32)
    for row in range(2 * NPOL):
        one = obs_ref[0, row]
        spread = jnp.concatenate([one] * (VT // quarter), axis=1)
        out_ref[4 + row : 5 + row, :] = jnp.where(mine, spread, 0.0)
    out_ref[12:16, :] = gain_first
    out_ref[16:20, :] = gain_second
    out_ref[20:22, :] = stations
    out_ref[22:23, :] = blocks_of
    out_ref[23:24, :] = channels


def slot_rows(where, table, observed, links, gains):
    smem = pl.BlockSpec(memory_space=pltpu.SMEM)
    anywhere = pl.BlockSpec(memory_space=pl.ANY)
    return pl.pallas_call(
        slots_kernel,
        out_shape=jax.ShapeDtypeStruct((24, VT), f32),
        in_specs=[smem, smem, pl.BlockSpec(memory_space=pltpu.VMEM), anywhere, anywhere],
        out_specs=pl.BlockSpec(memory_space=pltpu.VMEM),
        scratch_shapes=[
            pltpu.VMEM((NBLK, 2, LINK_WINDOW), jnp.int32),
            pltpu.VMEM((NBLK, 4, NST), f32),
            pltpu.SemaphoreType.DMA((NBLK,)),
            pltpu.SemaphoreType.DMA((NBLK,)),
        ],
        compiler_params=pltpu.CompilerParams(vmem_limit_bytes=8 * MIB),
        cost_estimate=pl.CostEstimate(flops=50_000_000, bytes_accessed=2 * MIB, transcendentals=0),
        name="slots",
    )(where, table, observed, *in_hbm(links, gains))


def predict_kernel(sc_ref, got_ref, b_ref, a_ref, info_ref, out_ref):
    rows = got_ref.shape[1]
    left = jnp.concatenate(
        [
            jnp.concatenate([got_ref[i * FGRID + j] for j in range(FGRID)], axis=1)
            for i in range(FGRID)
        ],
        axis=0,
    )
    del rows
    total_re = [jnp.zeros((1, VT), f32), jnp.zeros((1, VT), f32)]
    total_im = [jnp.zeros((1, VT), f32), jnp.zeros((1, VT), f32)]
    for w in range(NW):
        at = slice(w * 256, (w + 1) * 256)
        along_re = jnp.dot(left, b_ref[:, w * 256 : (w + 1) * 256], preferred_element_type=f32)
        along_im = jnp.dot(left, b_ref[:, 512 + w * 256 : 512 + (w + 1) * 256], preferred_element_type=f32)
        a_re = a_ref[0, :, at].astype(f32)
        a_im = a_ref[1, :, at].astype(f32)
        sum_re = jnp.sum(a_re * along_re - a_im * along_im, axis=0, keepdims=True)
        sum_im = jnp.sum(a_re * along_im + a_im * along_re, axis=0, keepdims=True)
        for side in range(2):
            total_re[side] = total_re[side] + sum_re[:, side * VT : (side + 1) * VT]
            total_im[side] = total_im[side] + sum_im[:, side * VT : (side + 1) * VT]
    first = sc_ref[2] == 0
    rows_out = [
        jnp.where(first, total_re[0], total_re[1]),
        jnp.where(first, total_re[1], total_re[0]),
        jnp.where(first, total_im[0], total_im[1]),
        jnp.where(first, total_im[1], total_im[0]),
    ]
    head = jnp.concatenate(rows_out + [info_ref[4:8, :]], axis=0)
    for to in range(out_ref.shape[0]):
        out_ref[to, 0:8, :] = head
        out_ref[to, 8:24, :] = info_ref[8:24, :]


def partial_predictions(where, got, b, a, info, peers):
    vmem = pl.BlockSpec(memory_space=pltpu.VMEM)
    return pl.pallas_call(
        predict_kernel,
        out_shape=jax.ShapeDtypeStruct((peers, 24, VT), f32),
        in_specs=[pl.BlockSpec(memory_space=pltpu.SMEM), vmem, vmem, vmem, vmem],
        out_specs=vmem,
        compiler_params=pltpu.CompilerParams(vmem_limit_bytes=20 * MIB),
        cost_estimate=pl.CostEstimate(flops=540_000_000, bytes_accessed=4 * MIB, transcendentals=0),
        name="predict",
    )(where, got, b, a, info)


def gradient_kernel(sc_ref, got_ref, resid_ref, out_ref):
    owners = 2
    own_class = sc_ref[1] * owners + sc_ref[2]
    row_id = lax.broadcasted_iota(jnp.int32, (NST // 8, VT), 0)
    block_row = lax.broadcasted_iota(jnp.int32, (VT, VT), 0) >> 2
    channels = got_ref[0, 23:24, :] + got_ref[1, 23:24, :]
    pick = lambda rows, order: jnp.concatenate([rows[i : i + 1] for i in order], axis=0)
    masks = {}
    values = {}
    resid_owner = []
    for o in range(owners):
        info = got_ref[o]
        measured = got_ref[o, 4:12, :]
        for p in range(1, NPOL):
            measured = measured + got_ref[p * owners + o, 4:12, :]
        pred_re = []
        pred_im = []
        for p in range(NPOL):
            one, two = got_ref[p * owners], got_ref[p * owners + 1]
            pred_re.append(one[o : o + 1] + two[o : o + 1])
            pred_im.append(one[2 + o : 3 + o] + two[2 + o : 3 + o])
        pred_re = jnp.concatenate(pred_re, axis=0)
        pred_im = jnp.concatenate(pred_im, axis=0)
        gain_first = info[12:16]
        gain_second = info[16:20]
        block = info[22:23].astype(jnp.int32)
        live = jnp.where(block >= 0, 1.0, 0.0)
        first_re = pick(gain_first, (0, 0, 2, 2))
        first_im = pick(gain_first, (1, 1, 3, 3))
        second_re = pick(gain_second, (0, 2, 0, 2))
        second_im = pick(gain_second, (1, 3, 1, 3))
        obs_re = pick(measured, (0, 2, 4, 6))
        obs_im = pick(measured, (1, 3, 5, 7))
        both_re = first_re * second_re + first_im * second_im
        both_im = first_im * second_re - first_re * second_im
        resid_re = live * (obs_re - (both_re * pred_re - both_im * pred_im))
        resid_im = live * (obs_im - (both_re * pred_im + both_im * pred_re))
        cross_re = second_re * pred_re + second_im * pred_im
        cross_im = second_im * pred_re - second_re * pred_im
        lead_re = -(resid_re * cross_re - resid_im * cross_im)
        lead_im = -(resid_re * cross_im + resid_im * cross_re)
        along_re = first_re * pred_re - first_im * pred_im
        along_im = first_re * pred_im + first_im * pred_re
        trail_re = -(resid_re * along_re + resid_im * along_im)
        trail_im = -(resid_re * along_im - resid_im * along_re)
        leading = jnp.concatenate(
            [
                lead_re[0:1] + lead_re[1:2],
                lead_im[0:1] + lead_im[1:2],
                lead_re[2:3] + lead_re[3:4],
                lead_im[2:3] + lead_im[3:4],
            ],
            axis=0,
        )
        trailing = jnp.concatenate(
            [
                trail_re[0:1] + trail_re[2:3],
                trail_im[0:1] + trail_im[2:3],
                trail_re[1:2] + trail_re[3:4],
                trail_im[1:2] + trail_im[3:4],
            ],
            axis=0,
        )
        resid_owner.append(
            jnp.concatenate(
                [r for p in range(NPOL) for r in (resid_re[p : p + 1], resid_im[p : p + 1])], axis=0
            )
        )
        chosen = block_row == jnp.where(block >= 0, NBLK * o + block, -1)
        for side, terms in ((0, leading), (1, trailing)):
            station = info[20 + side : 21 + side].astype(jnp.int32)
            key = jnp.where((station & 7) == own_class, station >> 3, -1)
            masks[side, o] = jnp.where(row_id == key, 1.0, 0.0).astype(bf16)
            tall = jnp.concatenate([terms, terms], axis=0)
            tall = jnp.concatenate([tall] * 16, axis=0)
            values[side, o] = jnp.where(chosen, tall, 0.0).astype(bf16)
    order = [(side, o) for side in range(2) for o in range(owners)]
    mask = jnp.concatenate([masks[at] for at in order], axis=1)
    value = jnp.concatenate([values[at] for at in order], axis=1)
    out_ref[...] = dot_nt(mask, value) + channels
    mine = jnp.where(sc_ref[2] == 0, resid_owner[0], resid_owner[1])
    resid_ref[...] = mine


def gradient_rows(where, got):
    vmem = pl.BlockSpec(memory_space=pltpu.VMEM)
    return pl.pallas_call(
        gradient_kernel,
        out_shape=(
            pltpu.VMEM((2 * NPOL, VT), f32),
            pltpu.VMEM((NST // 8, 128), f32),
        ),
        in_specs=[pl.BlockSpec(memory_space=pltpu.SMEM), vmem],
        out_specs=(vmem, vmem),
        compiler_params=pltpu.CompilerParams(vmem_limit_bytes=12 * MIB),
        cost_estimate=pl.CostEstimate(flops=70_000_000, bytes_accessed=MIB, transcendentals=0),
        name="gradient",
    )(where, got)


def collect_kernel(sc_ref, got_ref, mine_ref, out_hbm, resid_hbm, out_ref, resid_ref, sem):
    mine = mine_ref[...]
    quarter = resid_ref.shape[3]
    part = mine[:, 0:quarter]
    for q in range(1, NPOL):
        part = jnp.where(sc_ref[1] == q, mine[:, q * quarter : (q + 1) * quarter], part)
    for row in range(2 * NPOL):
        resid_ref[0, row] = part[row : row + 1, :]
    resid_copy = pltpu.make_async_copy(resid_ref, resid_hbm, sem.at[0])
    resid_copy.start()
    turned = got_ref[...].T
    lanes = turned.shape[1]
    channel_row = lax.broadcasted_iota(jnp.int32, (128, lanes), 0) >> 2
    group_row = lax.broadcasted_iota(jnp.int32, (8, lanes), 0)
    values = []
    groups = []
    for block in range(2 * NBLK):
        channel = turned[64 + block : 65 + block].astype(jnp.int32)
        terms = turned[4 * block : 4 * block + 4]
        tall = jnp.concatenate([terms, terms], axis=0)
        tall = jnp.concatenate([tall] * 16, axis=0)
        value = jnp.where(channel_row == (channel & 31), tall, 0.0).astype(bf16)
        group = jnp.where(group_row == (channel >> 5), 1.0, 0.0).astype(bf16)
        values.append(value)
        groups.append(group)
    total = dot_nt(jnp.concatenate(groups, axis=1), jnp.concatenate(values, axis=1))
    out_ref[...] = grad_scale * total
    out_copy = pltpu.make_async_copy(out_ref, out_hbm, sem.at[1])
    out_copy.start()
    out_copy.wait()
    resid_copy.wait()


def collect_rows(where, got, mine, quarter):
    vmem = pl.BlockSpec(memory_space=pltpu.VMEM)
    return pl.pallas_call(
        collect_kernel,
        out_shape=(
            jax.ShapeDtypeStruct((8, 128), f32),
            jax.ShapeDtypeStruct((1, 2 * NPOL, 1, quarter), f32),
        ),
        in_specs=[pl.BlockSpec(memory_space=pltpu.SMEM), vmem, vmem],
        out_specs=(pl.BlockSpec(memory_space=pl.ANY),) * 2,
        scratch_shapes=[
            pltpu.VMEM((8, 128), f32),
            pltpu.VMEM((1, 2 * NPOL, 1, quarter), f32),
            pltpu.SemaphoreType.DMA((2,)),
        ],
        compiler_params=pltpu.CompilerParams(vmem_limit_bytes=8 * MIB),
        cost_estimate=pl.CostEstimate(flops=2_000_000, bytes_accessed=65536, transcendentals=0),
        name="collect",
    )(where, got, mine)


def on_device(
    tile_spectral_lines,
    taper_leading_axis,
    taper_trailing_axis,
    depth_layer_factors,
    measured_correlations,
    visibility_groups_table,
    antenna_links,
    complex_receiver_factors,
):
    where = jnp.stack([lax.axis_index("facet"), lax.axis_index("pol"), lax.axis_index("tm")]).astype(jnp.int32)
    quarter = measured_correlations.shape[3]
    u = taper_leading_axis.reshape(VT, SG)
    v = taper_trailing_axis.reshape(VT, SG)
    w = depth_layer_factors.reshape(NW, VT)
    x = tile_spectral_lines.reshape(tile_spectral_lines.shape[2:])
    contrib, pack = contributions(x, u, v, w)
    received = lax.all_to_all(contrib, "facet", split_axis=0, concat_axis=0, tiled=True)
    other = lax.ppermute(pack, "tm", [(0, 1), (1, 0)])
    b, a = taper_transforms(where, pack, other)
    info = slot_rows(
        where,
        visibility_groups_table.reshape(3, NBLK),
        measured_correlations,
        antenna_links,
        complex_receiver_factors,
    )
    peers = lax.axis_size(("pol", "tm"))
    sent = partial_predictions(where, received, b, a, info, peers)
    gathered = lax.all_to_all(sent, ("pol", "tm"), split_axis=0, concat_axis=0, tiled=True)
    mine, partial_rows = gradient_rows(where, gathered)
    rows = lax.all_to_all(
        partial_rows.reshape(NST // 8, 1, 128), "facet", split_axis=0, concat_axis=0, tiled=True
    )
    gain_grad, residual = collect_rows(where, rows.reshape(NST // 8, 128), mine, quarter)
    return (residual, gain_grad.reshape(1, 4 * NCH))


def solution(mesh):
    return jax.shard_map(
        on_device,
        mesh=mesh,
        in_specs=(
            P("facet", "pol", None, "tm", None),
            P("facet", "tm", None, None),
            P("facet", "tm", None, None),
            P("facet", "tm", None, None),
            P("facet", None, "tm", "pol"),
            P("facet", "tm", None, None),
            P(),
            P(),
        ),
        out_specs=(P("facet", None, "tm", "pol"), P(("facet", "pol", "tm"), None)),
        check_vma=False,
    )
```

```python
import functools
import math

import jax
import jax.numpy as jnp
import ml_dtypes
import numpy as np
from jax import lax
from jax.experimental import pallas as pl
from jax.experimental.pallas import tpu as pltpu
from jax.sharding import PartitionSpec as P

FGRID = 8
FS = 4096
MC = 64
SG = 512
NPOL = 4
NW = 2
NCH = 256
NST = 512
VT = 128
NBLK = 8
LINK_WINDOW = 256
BATCHES = 2

w_chirp = 0.37
grad_scale = 0.1
MIB = 1 << 20

bf16 = jnp.bfloat16
f32 = jnp.float32
NT = (((1,), (1,)), ((), ()))


def dot_nt(left, right):
    return lax.dot_general(left, right, NT, preferred_element_type=f32)


def np_bf16(table):
    return np.asarray(table, np.float64).astype(np.float32).astype(ml_dtypes.bfloat16)


@functools.cache
def section_tables():
    a = np.arange(32)
    angle = -2 * np.pi * ((a[:, None] * a[None, :]) % 32) / 32
    c, s = np.cos(angle), np.sin(angle)
    first = np.block([[c, -s], [s, c]])
    k = np.arange(64)[:, None]
    l = np.arange(128)[None, :]
    turn = -2 * np.pi * ((k * l) % FS) / FS
    sub = np.arange(64)[:, None]
    angle = -2 * np.pi * ((sub * l) % 64) / 64
    last = np.concatenate([np.cos(angle), np.sin(angle)], axis=1) / math.sqrt(FS)
    return (
        np_bf16(first),
        np.stack([np.cos(turn), np.sin(turn)]).astype(np.float32),
        np_bf16(last),
    )


@functools.cache
def taper_tables():
    x = np.arange(SG)
    angle = 2 * np.pi * ((x[:, None] * x[None, :]) % SG) / SG
    table = np.exp(1j * angle) / math.sqrt(SG)
    across = (x - SG // 2) ** 2 * (w_chirp / SG**2)
    trailing, leading = [], []
    for w in range(NW):
        full = table * np.exp(2j * np.pi * w * across)[None, :]
        rows = np.stack([full.real, -full.imag]).reshape(2, FGRID, MC, SG)
        trailing.append(rows.transpose(1, 0, 2, 3).reshape(2 * SG, SG))
        halves = np.stack([full.real, full.imag]).reshape(2, FGRID, 2, MC // 2, SG)
        leading.append(halves.transpose(2, 0, 1, 3, 4).reshape(2, 2 * SG // 2, SG))
    return np_bf16(np.stack(trailing)), np_bf16(np.stack(leading, axis=1))


def in_hbm(*arrays):
    return [pltpu.with_memory_space_constraint(one, pltpu.HBM) for one in arrays]


def contrib_kernel(
    x_hbm, u_hbm, v_hbm, w_hbm, first_hbm, turn_hbm, last_hbm,
    out_hbm, pack_ref,
    x_ref, w_ref, first_ref, turn_ref, last_ref, spread, lined, placed, out_ref, x_sem, sem, out_sem,
):
    rows = x_ref.shape[1]
    batch = rows // BATCHES
    pieces = [
        pltpu.make_async_copy(
            x_hbm.at[:, pl.ds(h * batch, batch), :], x_ref.at[:, pl.ds(h * batch, batch), :], x_sem.at[h]
        )
        for h in range(BATCHES)
    ]
    tables = [
        pltpu.make_async_copy(source, target, sem.at[i])
        for i, (source, target) in enumerate(
            ((first_hbm, first_ref), (turn_hbm, turn_ref), (last_hbm, last_ref))
        )
    ]
    tapers = [
        pltpu.make_async_copy(source, target, sem.at[3 + i])
        for i, (source, target) in enumerate(
            (
                (w_hbm, w_ref),
                (u_hbm, pack_ref.at[pl.ds(0, VT), :]),
                (v_hbm, pack_ref.at[pl.ds(VT, VT), :]),
            )
        )
    ]
    results = [
        pltpu.make_async_copy(out_ref.at[h], out_hbm.at[:, pl.ds(h * batch, batch), :], out_sem.at[h])
        for h in range(BATCHES)
    ]
    for copy in pieces[:1] + tables + pieces[1:] + tapers:
        copy.start()

    def section_of(pair):
        return jnp.dot(first_ref[...], lined[:, pair * 256 : (pair + 1) * 256], preferred_element_type=f32)

    def turned_of(section):
        turn_re = turn_ref[0]
        turn_im = turn_ref[1]
        sides = []
        for half in range(2):
            one = section[:, half * 128 : (half + 1) * 128]
            re = jnp.concatenate([one[0:32], one[0:32]], axis=0)
            im = jnp.concatenate([one[32:64], one[32:64]], axis=0)
            turned_re = (re * turn_re - im * turn_im).astype(bf16)
            turned_im = (re * turn_im + im * turn_re).astype(bf16)
            sides.append(
                jnp.concatenate(
                    [
                        jnp.concatenate([turned_re, -turned_im], axis=1),
                        jnp.concatenate([turned_im, turned_re], axis=1),
                    ],
                    axis=0,
                )
            )
        return jnp.concatenate(sides, axis=0)

    def finish(pair, turned):
        result = dot_nt(last_ref[...], turned)
        placed[pl.ds(2 * pair, 64, stride=rows), :] = result[:, 0:128]
        placed[pl.ds(2 * pair + 1, 64, stride=rows), :] = result[:, 128:256]

    def line_up(h):
        pieces[h].wait()
        for part in range(2):
            for a in range(32):
                at = (part * 32 + a) * rows + h * batch
                spread[at : at + batch, :] = x_ref[
                    part, h * batch : (h + 1) * batch, a * 128 : (a + 1) * 128
                ].astype(f32)
        for m in range(h * batch, (h + 1) * batch):
            lined[:, m * 128 : (m + 1) * 128] = spread[pl.ds(m, 64, stride=rows), :].astype(bf16)

    def send(h):
        for s in range(64):
            at = s * rows + h * batch
            out_ref[h, s] = placed[at : at + batch, :].astype(bf16)
        results[h].start()

    per = batch // 2
    line_up(0)
    for copy in tables:
        copy.wait()
    pairs = rows // 2
    sections = {0: section_of(0), 1: section_of(1)}
    turned = {}
    for step in range(pairs + 1):
        if step + 2 < pairs:
            if (step + 2) % per == 0:
                line_up((step + 2) // per)
            sections[step + 2] = section_of(step + 2)
        if step < pairs:
            turned[step] = turned_of(sections.pop(step))
        if step >= 1:
            finish(step - 1, turned.pop(step - 1))
            if step % per == 0:
                send(step // per - 1)
    for copy in tapers:
        copy.wait()
    weights = jnp.concatenate([w_ref[...].astype(f32), jnp.zeros((16 - NW, VT), f32)], axis=0).astype(bf16)
    pack_ref[2 * VT : 2 * VT + 16, :] = jnp.concatenate([weights] * (SG // VT), axis=1)
    for copy in results:
        copy.wait()


def contributions(x, u, v, w):
    rows = x.shape[1]
    first, turn, last = section_tables()
    anywhere = pl.BlockSpec(memory_space=pl.ANY)
    vmem = pl.BlockSpec(memory_space=pltpu.VMEM)
    return pl.pallas_call(
        contrib_kernel,
        out_shape=(
            jax.ShapeDtypeStruct((64, rows, 128), bf16),
            pltpu.VMEM((2 * VT + 16, SG), bf16),
        ),
        in_specs=[anywhere] * 7,
        out_specs=(anywhere, vmem),
        scratch_shapes=[
            pltpu.VMEM((2, rows, FS), bf16),
            pltpu.VMEM((NW, VT), bf16),
            pltpu.VMEM((64, 64), bf16),
            pltpu.VMEM((2, 64, 128), f32),
            pltpu.VMEM((64, 256), bf16),
            pltpu.VMEM((64 * rows, 128), f32),
            pltpu.VMEM((64, 128 * rows), bf16),
            pltpu.VMEM((64 * rows, 128), f32),
            pltpu.VMEM((BATCHES, 64, rows // BATCHES, 128), bf16),
            pltpu.SemaphoreType.DMA((BATCHES,)),
            pltpu.SemaphoreType.DMA((6,)),
            pltpu.SemaphoreType.DMA((BATCHES,)),
        ],
        compiler_params=pltpu.CompilerParams(vmem_limit_bytes=16 * MIB),
        cost_estimate=pl.CostEstimate(flops=300_000_000, bytes_accessed=2 * MIB, transcendentals=0),
        name="contrib",
    )(*in_hbm(x, u, v, w, jnp.asarray(first), jnp.asarray(turn), jnp.asarray(last)))


def taper_kernel(sc_ref, own_ref, other_ref, trail_hbm, lead_hbm, b_ref, a_ref, trail_ref, lead_ref, sem):
    trail_copies = [
        pltpu.make_async_copy(trail_hbm.at[w], trail_ref.at[w], sem.at[w]) for w in range(NW)
    ]
    lead_copies = [
        pltpu.make_async_copy(lead_hbm.at[sc_ref[2], w], lead_ref.at[w], sem.at[NW + w]) for w in range(NW)
    ]
    for copy in trail_copies + lead_copies:
        copy.start()
    v_all = jnp.concatenate([own_ref[VT : 2 * VT, :], other_ref[VT : 2 * VT, :]], axis=0)
    u_all = jnp.concatenate([own_ref[0:VT, :], other_ref[0:VT, :]], axis=0)
    weights = jnp.concatenate(
        [own_ref[2 * VT : 2 * VT + 16, 0:VT], other_ref[2 * VT : 2 * VT + 16, 0:VT]], axis=1
    ).astype(f32)
    for w in range(NW):
        trail_copies[w].wait()
        re_at = slice(w * 256, (w + 1) * 256)
        im_at = slice(512 + w * 256, 512 + (w + 1) * 256)
        for j in range(FGRID):
            got = dot_nt(trail_ref[w, j * 128 : (j + 1) * 128, :], v_all)
            b_ref[j * 128 : (j + 1) * 128, re_at] = got.astype(bf16)
            b_ref[j * 128 : j * 128 + 64, im_at] = (-got[64:128]).astype(bf16)
            b_ref[j * 128 + 64 : (j + 1) * 128, im_at] = got[0:64].astype(bf16)
    for w in range(NW):
        lead_copies[w].wait()
        re_at = slice(w * 256, (w + 1) * 256)
        scale = weights[w : w + 1, :]
        a_ref[0, :, re_at] = (dot_nt(lead_ref[w, 0:256, :], u_all) * scale).astype(bf16)
        a_ref[1, :, re_at] = (dot_nt(lead_ref[w, 256:512, :], u_all) * scale).astype(bf16)


def taper_transforms(where, own, other):
    trailing, leading = taper_tables()
    anywhere = pl.BlockSpec(memory_space=pl.ANY)
    vmem = pl.BlockSpec(memory_space=pltpu.VMEM)
    return pl.pallas_call(
        taper_kernel,
        out_shape=(
            pltpu.VMEM((2 * SG, 1024), bf16),
            pltpu.VMEM((2, SG // 2, 512), bf16),
        ),
        in_specs=[pl.BlockSpec(memory_space=pltpu.SMEM), vmem, vmem, anywhere, anywhere],
        out_specs=(vmem, vmem),
        scratch_shapes=[
            pltpu.VMEM((NW, 2 * SG, SG), bf16),
            pltpu.VMEM((NW, SG, SG), bf16),
            pltpu.SemaphoreType.DMA((2 * NW,)),
        ],
        compiler_params=pltpu.CompilerParams(vmem_limit_bytes=24 * MIB),
        cost_estimate=pl.CostEstimate(flops=800_000_000, bytes_accessed=8 * MIB, transcendentals=0),
        name="tapers",
    )(where, own, other, *in_hbm(jnp.asarray(trailing), jnp.asarray(leading)))


def slots_kernel(sc_ref, table_ref, obs_ref, links_ref, gains_ref, out_ref, window, factors, link_sem, gain_sem):
    tiles = links_ref.shape[1] // 128
    begin = jnp.int32(0)
    blocks = []
    copies = []
    for b in range(NBLK):
        channel = table_ref[0, b]
        offset = table_ref[1, b]
        amount = table_ref[2, b]
        tile = jnp.minimum(offset // 128, tiles - LINK_WINDOW // 128)
        at = pl.multiple_of(tile * 128, 128)
        copies.append(
            pltpu.make_async_copy(links_ref.at[:, pl.ds(at, LINK_WINDOW)], window.at[b], link_sem.at[b])
        )
        copies.append(pltpu.make_async_copy(gains_ref.at[channel], factors.at[b], gain_sem.at[b]))
        blocks.append((channel, offset - at, amount, begin))
        begin = begin + amount
    for copy in copies:
        copy.start()
    slot = lax.broadcasted_iota(jnp.int32, (1, VT), 1)
    members = []
    chooser = []
    blocks_of = jnp.full((1, VT), -1.0, f32)
    channels = jnp.zeros((1, VT), f32)
    index = lax.broadcasted_iota(jnp.int32, (LINK_WINDOW, VT), 0)
    for b, (channel, shift, amount, start) in enumerate(blocks):
        inside = (slot >= start) & (slot < start + amount)
        member = jnp.where(inside, 1.0, 0.0)
        members.append(member)
        blocks_of = jnp.where(inside, float(b), blocks_of)
        channels = jnp.where(slot == NBLK * sc_ref[2] + (64 + b), channel.astype(f32), channels)
        want = jnp.where(inside, slot - start + shift, -1)
        chooser.append(jnp.where(index == want, 1.0, 0.0).astype(bf16))
    for copy in copies:
        copy.wait()
    digits = []
    for b in range(NBLK):
        found = window[b]
        high = found >> 4
        digits.append(jnp.concatenate([high, found - (high << 4)], axis=0).astype(f32).astype(bf16))
    picked = jnp.dot(
        jnp.concatenate(digits, axis=1), jnp.concatenate(chooser, axis=0), preferred_element_type=f32
    )
    stations = picked[0:2] * 16.0 + picked[2:4]
    both = jnp.concatenate([stations[0:1], stations[1:2]], axis=1).astype(jnp.int32)
    station_index = lax.broadcasted_iota(jnp.int32, (NST, 2 * VT), 0)
    onehot = jnp.where(station_index == both, 1.0, 0.0).astype(bf16)
    rest = jnp.concatenate([factors[b] for b in range(NBLK)], axis=0)
    taken = jnp.zeros((4 * NBLK, 2 * VT), f32)
    for piece in range(3):
        rounded = rest.astype(bf16)
        taken = taken + jnp.dot(rounded, onehot, preferred_element_type=f32)
        rest = rest - rounded.astype(f32)
    gain_first = jnp.zeros((4, VT), f32)
    gain_second = jnp.zeros((4, VT), f32)
    for b in range(NBLK):
        gain_first = gain_first + members[b] * taken[4 * b : 4 * b + 4, 0:VT]
        gain_second = gain_second + members[b] * taken[4 * b : 4 * b + 4, VT : 2 * VT]
    quarter = obs_ref.shape[3]
    lane = lax.broadcasted_iota(jnp.int32, (1, VT), 1)
    mine = (lane // quarter) == sc_ref[1]
    out_ref[0:1, :] = jnp.full((1, VT), sc_ref[2].astype(f32))
    out_ref[1:2, :] = jnp.full((1, VT), sc_ref[1].astype(f32))
    out_ref[2:4, :] = jnp.zeros((2, VT), f32)
    for row in range(2 * NPOL):
        one = obs_ref[0, row]
        spread = jnp.concatenate([one] * (VT // quarter), axis=1)
        out_ref[4 + row : 5 + row, :] = jnp.where(mine, spread, 0.0)
    out_ref[12:16, :] = gain_first
    out_ref[16:20, :] = gain_second
    out_ref[20:22, :] = stations
    out_ref[22:23, :] = blocks_of
    out_ref[23:24, :] = channels


def slot_rows(where, table, observed, links, gains):
    smem = pl.BlockSpec(memory_space=pltpu.SMEM)
    anywhere = pl.BlockSpec(memory_space=pl.ANY)
    return pl.pallas_call(
        slots_kernel,
        out_shape=jax.ShapeDtypeStruct((24, VT), f32),
        in_specs=[smem, smem, pl.BlockSpec(memory_space=pltpu.VMEM), anywhere, anywhere],
        out_specs=pl.BlockSpec(memory_space=pltpu.VMEM),
        scratch_shapes=[
            pltpu.VMEM((NBLK, 2, LINK_WINDOW), jnp.int32),
            pltpu.VMEM((NBLK, 4, NST), f32),
            pltpu.SemaphoreType.DMA((NBLK,)),
            pltpu.SemaphoreType.DMA((NBLK,)),
        ],
        compiler_params=pltpu.CompilerParams(vmem_limit_bytes=8 * MIB),
        cost_estimate=pl.CostEstimate(flops=50_000_000, bytes_accessed=2 * MIB, transcendentals=0),
        name="slots",
    )(where, table, observed, *in_hbm(links, gains))


def predict_kernel(got_ref, b_ref, a_ref, info_ref, out_ref):
    rows = got_ref.shape[1]
    left = jnp.concatenate(
        [
            jnp.concatenate([got_ref[i * FGRID + j] for j in range(FGRID)], axis=1)
            for i in range(FGRID)
        ],
        axis=0,
    )
    del rows
    total_re = [jnp.zeros((1, VT), f32), jnp.zeros((1, VT), f32)]
    total_im = [jnp.zeros((1, VT), f32), jnp.zeros((1, VT), f32)]
    for w in range(NW):
        at = slice(w * 256, (w + 1) * 256)
        along_re = jnp.dot(left, b_ref[:, w * 256 : (w + 1) * 256], preferred_element_type=f32)
        along_im = jnp.dot(left, b_ref[:, 512 + w * 256 : 512 + (w + 1) * 256], preferred_element_type=f32)
        a_re = a_ref[0, :, at].astype(f32)
        a_im = a_ref[1, :, at].astype(f32)
        sum_re = jnp.sum(a_re * along_re - a_im * along_im, axis=0, keepdims=True)
        sum_im = jnp.sum(a_re * along_im + a_im * along_re, axis=0, keepdims=True)
        for side in range(2):
            total_re[side] = total_re[side] + sum_re[:, side * VT : (side + 1) * VT]
            total_im[side] = total_im[side] + sum_im[:, side * VT : (side + 1) * VT]
    first = info_ref[0:1, :] == 0.0
    rows_out = [
        jnp.where(first, total_re[0], total_re[1]),
        jnp.where(first, total_re[1], total_re[0]),
        jnp.where(first, total_im[0], total_im[1]),
        jnp.where(first, total_im[1], total_im[0]),
    ]
    head = jnp.concatenate(rows_out + [info_ref[4:8, :]], axis=0)
    for to in range(out_ref.shape[0]):
        out_ref[to, 0:8, :] = head
        out_ref[to, 8:24, :] = info_ref[8:24, :]


def partial_predictions(got, b, a, info, peers):
    vmem = pl.BlockSpec(memory_space=pltpu.VMEM)
    return pl.pallas_call(
        predict_kernel,
        out_shape=jax.ShapeDtypeStruct((peers, 24, VT), f32),
        in_specs=[vmem] * 4,
        out_specs=vmem,
        compiler_params=pltpu.CompilerParams(vmem_limit_bytes=20 * MIB),
        cost_estimate=pl.CostEstimate(flops=540_000_000, bytes_accessed=4 * MIB, transcendentals=0),
        name="predict",
    )(got, b, a, info)


def gradient_kernel(info_ref, got_ref, resid_ref, out_ref):
    owners = 2
    own_tm = info_ref[0:1, :]
    own_pol = info_ref[1:2, :]
    own_class = (own_pol * owners + own_tm).astype(jnp.int32)
    row_id = lax.broadcasted_iota(jnp.int32, (NST // 8, VT), 0)
    block_row = lax.broadcasted_iota(jnp.int32, (VT, VT), 0) >> 2
    channels = got_ref[0, 23:24, :] + got_ref[1, 23:24, :]
    pick = lambda rows, order: jnp.concatenate([rows[i : i + 1] for i in order], axis=0)
    masks = {}
    values = {}
    resid_owner = []
    for o in range(owners):
        info = got_ref[o]
        measured = got_ref[o, 4:12, :]
        for p in range(1, NPOL):
            measured = measured + got_ref[p * owners + o, 4:12, :]
        pred_re = []
        pred_im = []
        for p in range(NPOL):
            one, two = got_ref[p * owners], got_ref[p * owners + 1]
            pred_re.append(one[o : o + 1] + two[o : o + 1])
            pred_im.append(one[2 + o : 3 + o] + two[2 + o : 3 + o])
        pred_re = jnp.concatenate(pred_re, axis=0)
        pred_im = jnp.concatenate(pred_im, axis=0)
        gain_first = info[12:16]
        gain_second = info[16:20]
        block = info[22:23].astype(jnp.int32)
        live = jnp.where(block >= 0, 1.0, 0.0)
        first_re = pick(gain_first, (0, 0, 2, 2))
        first_im = pick(gain_first, (1, 1, 3, 3))
        second_re = pick(gain_second, (0, 2, 0, 2))
        second_im = pick(gain_second, (1, 3, 1, 3))
        obs_re = pick(measured, (0, 2, 4, 6))
        obs_im = pick(measured, (1, 3, 5, 7))
        both_re = first_re * second_re + first_im * second_im
        both_im = first_im * second_re - first_re * second_im
        resid_re = live * (obs_re - (both_re * pred_re - both_im * pred_im))
        resid_im = live * (obs_im - (both_re * pred_im + both_im * pred_re))
        cross_re = second_re * pred_re + second_im * pred_im
        cross_im = second_im * pred_re - second_re * pred_im
        lead_re = -(resid_re * cross_re - resid_im * cross_im)
        lead_im = -(resid_re * cross_im + resid_im * cross_re)
        along_re = first_re * pred_re - first_im * pred_im
        along_im = first_re * pred_im + first_im * pred_re
        trail_re = -(resid_re * along_re + resid_im * along_im)
        trail_im = -(resid_re * along_im - resid_im * along_re)
        leading = jnp.concatenate(
            [
                lead_re[0:1] + lead_re[1:2],
                lead_im[0:1] + lead_im[1:2],
                lead_re[2:3] + lead_re[3:4],
                lead_im[2:3] + lead_im[3:4],
            ],
            axis=0,
        )
        trailing = jnp.concatenate(
            [
                trail_re[0:1] + trail_re[2:3],
                trail_im[0:1] + trail_im[2:3],
                trail_re[1:2] + trail_re[3:4],
                trail_im[1:2] + trail_im[3:4],
            ],
            axis=0,
        )
        resid_owner.append(
            jnp.concatenate(
                [r for p in range(NPOL) for r in (resid_re[p : p + 1], resid_im[p : p + 1])], axis=0
            )
        )
        chosen = block_row == jnp.where(block >= 0, NBLK * o + block, -1)
        for side, terms in ((0, leading), (1, trailing)):
            station = info[20 + side : 21 + side].astype(jnp.int32)
            key = jnp.where((station & 7) == own_class, station >> 3, -1)
            masks[side, o] = jnp.where(row_id == key, 1.0, 0.0).astype(bf16)
            tall = jnp.concatenate([terms, terms], axis=0)
            tall = jnp.concatenate([tall] * 16, axis=0)
            values[side, o] = jnp.where(chosen, tall, 0.0).astype(bf16)
    order = [(side, o) for side in range(2) for o in range(owners)]
    mask = jnp.concatenate([masks[at] for at in order], axis=1)
    value = jnp.concatenate([values[at] for at in order], axis=1)
    out_ref[...] = dot_nt(mask, value) + channels
    mine = jnp.where(own_tm == 0.0, resid_owner[0], resid_owner[1])
    quarter = resid_ref.shape[1]
    part = mine[:, 0:quarter]
    for q in range(1, NPOL):
        part = jnp.where(own_pol[:, 0:quarter] == float(q), mine[:, q * quarter : (q + 1) * quarter], part)
    resid_ref[...] = part


def gradient_rows(info, got):
    vmem = pl.BlockSpec(memory_space=pltpu.VMEM)
    return pl.pallas_call(
        gradient_kernel,
        out_shape=(
            pltpu.VMEM((2 * NPOL, VT // NPOL), f32),
            pltpu.VMEM((NST // 8, 128), f32),
        ),
        in_specs=[vmem, vmem],
        out_specs=(vmem, vmem),
        compiler_params=pltpu.CompilerParams(vmem_limit_bytes=12 * MIB),
        cost_estimate=pl.CostEstimate(flops=70_000_000, bytes_accessed=MIB, transcendentals=0),
        name="gradient",
    )(info, got)


def collect_kernel(got_ref, mine_ref, out_hbm, resid_hbm, out_ref, resid_ref, sem):
    part = mine_ref[...]
    for row in range(2 * NPOL):
        resid_ref[0, row] = part[row : row + 1, :]
    resid_copy = pltpu.make_async_copy(resid_ref, resid_hbm, sem.at[0])
    resid_copy.start()
    turned = got_ref[...].T
    lanes = turned.shape[1]
    channel_row = lax.broadcasted_iota(jnp.int32, (128, lanes), 0) >> 2
    group_row = lax.broadcasted_iota(jnp.int32, (8, lanes), 0)
    values = []
    groups = []
    for block in range(2 * NBLK):
        channel = turned[64 + block : 65 + block].astype(jnp.int32)
        terms = turned[4 * block : 4 * block + 4]
        tall = jnp.concatenate([terms, terms], axis=0)
        tall = jnp.concatenate([tall] * 16, axis=0)
        value = jnp.where(channel_row == (channel & 31), tall, 0.0).astype(bf16)
        group = jnp.where(group_row == (channel >> 5), 1.0, 0.0).astype(bf16)
        values.append(value)
        groups.append(group)
    total = dot_nt(jnp.concatenate(groups, axis=1), jnp.concatenate(values, axis=1))
    out_ref[...] = grad_scale * total
    out_copy = pltpu.make_async_copy(out_ref, out_hbm, sem.at[1])
    out_copy.start()
    out_copy.wait()
    resid_copy.wait()


def collect_rows(got, mine, quarter):
    vmem = pl.BlockSpec(memory_space=pltpu.VMEM)
    return pl.pallas_call(
        collect_kernel,
        out_shape=(
            jax.ShapeDtypeStruct((8, 128), f32),
            jax.ShapeDtypeStruct((1, 2 * NPOL, 1, quarter), f32),
        ),
        in_specs=[vmem, vmem],
        out_specs=(pl.BlockSpec(memory_space=pl.ANY),) * 2,
        scratch_shapes=[
            pltpu.VMEM((8, 128), f32),
            pltpu.VMEM((1, 2 * NPOL, 1, quarter), f32),
            pltpu.SemaphoreType.DMA((2,)),
        ],
        compiler_params=pltpu.CompilerParams(vmem_limit_bytes=8 * MIB),
        cost_estimate=pl.CostEstimate(flops=2_000_000, bytes_accessed=65536, transcendentals=0),
        name="collect",
    )(got, mine)


def on_device(
    tile_spectral_lines,
    taper_leading_axis,
    taper_trailing_axis,
    depth_layer_factors,
    measured_correlations,
    visibility_groups_table,
    antenna_links,
    complex_receiver_factors,
):
    where = jnp.stack([lax.axis_index("facet"), lax.axis_index("pol"), lax.axis_index("tm")]).astype(jnp.int32)
    quarter = measured_correlations.shape[3]
    u = taper_leading_axis.reshape(VT, SG)
    v = taper_trailing_axis.reshape(VT, SG)
    w = depth_layer_factors.reshape(NW, VT)
    x = tile_spectral_lines.reshape(tile_spectral_lines.shape[2:])
    contrib, pack = contributions(x, u, v, w)
    received = lax.all_to_all(contrib, "facet", split_axis=0, concat_axis=0, tiled=True)
    other = lax.ppermute(pack, "tm", [(0, 1), (1, 0)])
    b, a = taper_transforms(where, pack, other)
    info = slot_rows(
        where,
        visibility_groups_table.reshape(3, NBLK),
        measured_correlations,
        antenna_links,
        complex_receiver_factors,
    )
    peers = lax.axis_size(("pol", "tm"))
    sent = partial_predictions(received, b, a, info, peers)
    gathered = lax.all_to_all(sent, ("pol", "tm"), split_axis=0, concat_axis=0, tiled=True)
    mine, partial_rows = gradient_rows(info, gathered)
    rows = lax.all_to_all(
        partial_rows.reshape(NST // 8, 1, 128), "facet", split_axis=0, concat_axis=0, tiled=True
    )
    gain_grad, residual = collect_rows(rows.reshape(NST // 8, 128), mine, quarter)
    return (residual, gain_grad.reshape(1, 4 * NCH))


def solution(mesh):
    return jax.shard_map(
        on_device,
        mesh=mesh,
        in_specs=(
            P("facet", "pol", None, "tm", None),
            P("facet", "tm", None, None),
            P("facet", "tm", None, None),
            P("facet", "tm", None, None),
            P("facet", None, "tm", "pol"),
            P("facet", "tm", None, None),
            P(),
            P(),
        ),
        out_specs=(P("facet", None, "tm", "pol"), P(("facet", "pol", "tm"), None)),
        check_vma=False,
    )
```

```python
import functools
import math

import jax
import jax.numpy as jnp
import ml_dtypes
import numpy as np
from jax import lax
from jax.experimental import pallas as pl
from jax.experimental.pallas import tpu as pltpu
from jax.sharding import PartitionSpec as P

FGRID = 8
FS = 4096
MC = 64
SG = 512
NPOL = 4
NW = 2
NCH = 256
NST = 512
VT = 128
NBLK = 8
LINK_WINDOW = 256
BATCHES = 2
X_CUTS = 4

w_chirp = 0.37
grad_scale = 0.1
MIB = 1 << 20

bf16 = jnp.bfloat16
f32 = jnp.float32
NT = (((1,), (1,)), ((), ()))


def dot_nt(left, right):
    return lax.dot_general(left, right, NT, preferred_element_type=f32)


def np_bf16(table):
    return np.asarray(table, np.float64).astype(np.float32).astype(ml_dtypes.bfloat16)


@functools.cache
def section_tables():
    a = np.arange(32)
    angle = -2 * np.pi * ((a[:, None] * a[None, :]) % 32) / 32
    c, s = np.cos(angle), np.sin(angle)
    first = np.block([[c, -s], [s, c]])
    k = np.arange(64)[:, None]
    l = np.arange(128)[None, :]
    turn = -2 * np.pi * ((k * l) % FS) / FS
    sub = np.arange(64)[:, None]
    angle = -2 * np.pi * ((sub * l) % 64) / 64
    last = np.concatenate([np.cos(angle), np.sin(angle)], axis=1) / math.sqrt(FS)
    return (
        np_bf16(first),
        np.stack([np.cos(turn), np.sin(turn)]).astype(np.float32),
        np_bf16(last),
    )


@functools.cache
def taper_tables():
    x = np.arange(SG)
    angle = 2 * np.pi * ((x[:, None] * x[None, :]) % SG) / SG
    table = np.exp(1j * angle) / math.sqrt(SG)
    across = (x - SG // 2) ** 2 * (w_chirp / SG**2)
    trailing, leading = [], []
    for w in range(NW):
        full = table * np.exp(2j * np.pi * w * across)[None, :]
        rows = np.stack([full.real, -full.imag]).reshape(2, FGRID, MC, SG)
        trailing.append(rows.transpose(1, 0, 2, 3).reshape(2 * SG, SG))
        halves = np.stack([full.real, full.imag]).reshape(2, FGRID, 2, MC // 2, SG)
        leading.append(halves.transpose(2, 0, 1, 3, 4).reshape(2, 2 * SG // 2, SG))
    return np_bf16(np.stack(trailing)), np_bf16(np.stack(leading, axis=1))


def in_hbm(*arrays):
    return [pltpu.with_memory_space_constraint(one, pltpu.HBM) for one in arrays]


def contrib_kernel(
    x_hbm, u_hbm, v_hbm, w_hbm, first_hbm, turn_hbm, last_hbm,
    out_hbm, pack_ref,
    x_ref, w_ref, first_ref, turn_ref, last_ref, spread, lined, placed, out_ref, x_sem, sem, out_sem,
):
    rows = x_ref.shape[1]
    batch = rows // BATCHES
    wide = FS // X_CUTS
    pieces = [
        pltpu.make_async_copy(
            x_hbm.at[:, pl.ds(h * batch, batch), pl.ds(c * wide, wide)],
            x_ref.at[:, pl.ds(h * batch, batch), pl.ds(c * wide, wide)],
            x_sem.at[h, c],
        )
        for h in range(BATCHES)
        for c in range(X_CUTS)
    ]
    tables = [
        pltpu.make_async_copy(source, target, sem.at[i])
        for i, (source, target) in enumerate(
            ((first_hbm, first_ref), (turn_hbm, turn_ref), (last_hbm, last_ref))
        )
    ]
    tapers = [
        pltpu.make_async_copy(source, target, sem.at[3 + i])
        for i, (source, target) in enumerate(
            (
                (w_hbm, w_ref),
                (u_hbm, pack_ref.at[pl.ds(0, VT), :]),
                (v_hbm, pack_ref.at[pl.ds(VT, VT), :]),
            )
        )
    ]
    results = [
        pltpu.make_async_copy(out_ref.at[h], out_hbm.at[:, pl.ds(h * batch, batch), :], out_sem.at[h])
        for h in range(BATCHES)
    ]
    for copy in pieces[:X_CUTS] + tables + pieces[X_CUTS:]:
        copy.start()

    def section_of(pair):
        return jnp.dot(first_ref[...], lined[:, pair * 256 : (pair + 1) * 256], preferred_element_type=f32)

    def turned_of(section):
        turn_re = turn_ref[0]
        turn_im = turn_ref[1]
        sides = []
        for half in range(2):
            one = section[:, half * 128 : (half + 1) * 128]
            re = jnp.concatenate([one[0:32], one[0:32]], axis=0)
            im = jnp.concatenate([one[32:64], one[32:64]], axis=0)
            turned_re = (re * turn_re - im * turn_im).astype(bf16)
            turned_im = (re * turn_im + im * turn_re).astype(bf16)
            sides.append(
                jnp.concatenate(
                    [
                        jnp.concatenate([turned_re, -turned_im], axis=1),
                        jnp.concatenate([turned_im, turned_re], axis=1),
                    ],
                    axis=0,
                )
            )
        return jnp.concatenate(sides, axis=0)

    def finish(pair, turned):
        result = dot_nt(last_ref[...], turned)
        placed[pl.ds(2 * pair, 64, stride=rows), :] = result[:, 0:128]
        placed[pl.ds(2 * pair + 1, 64, stride=rows), :] = result[:, 128:256]

    def line_up(h):
        for c in range(X_CUTS):
            pieces[h * X_CUTS + c].wait()
            take(h, c)
        for m in range(h * batch, (h + 1) * batch):
            lined[:, m * 128 : (m + 1) * 128] = spread[pl.ds(m, 64, stride=rows), :].astype(bf16)

    def take(h, c):
        for part in range(2):
            for a in range(c * 32 // X_CUTS, (c + 1) * 32 // X_CUTS):
                at = (part * 32 + a) * rows + h * batch
                spread[at : at + batch, :] = x_ref[
                    part, h * batch : (h + 1) * batch, a * 128 : (a + 1) * 128
                ].astype(f32)

    def send(h):
        for s in range(64):
            at = s * rows + h * batch
            out_ref[h, s] = placed[at : at + batch, :].astype(bf16)
        results[h].start()

    per = batch // 2
    line_up(0)
    for copy in tapers:
        copy.start()
    for copy in tables:
        copy.wait()
    pairs = rows // 2
    sections = {0: section_of(0), 1: section_of(1)}
    turned = {}
    for step in range(pairs + 1):
        if step + 2 < pairs:
            if (step + 2) % per == 0:
                line_up((step + 2) // per)
            sections[step + 2] = section_of(step + 2)
        if step < pairs:
            turned[step] = turned_of(sections.pop(step))
        if step >= 1:
            finish(step - 1, turned.pop(step - 1))
            if step % per == 0:
                send(step // per - 1)
    for copy in tapers:
        copy.wait()
    weights = jnp.concatenate([w_ref[...].astype(f32), jnp.zeros((16 - NW, VT), f32)], axis=0).astype(bf16)
    pack_ref[2 * VT : 2 * VT + 16, :] = jnp.concatenate([weights] * (SG // VT), axis=1)
    for copy in results:
        copy.wait()


def contributions(x, u, v, w):
    rows = x.shape[1]
    first, turn, last = section_tables()
    anywhere = pl.BlockSpec(memory_space=pl.ANY)
    vmem = pl.BlockSpec(memory_space=pltpu.VMEM)
    return pl.pallas_call(
        contrib_kernel,
        out_shape=(
            jax.ShapeDtypeStruct((64, rows, 128), bf16),
            pltpu.VMEM((2 * VT + 16, SG), bf16),
        ),
        in_specs=[anywhere] * 7,
        out_specs=(anywhere, vmem),
        scratch_shapes=[
            pltpu.VMEM((2, rows, FS), bf16),
            pltpu.VMEM((NW, VT), bf16),
            pltpu.VMEM((64, 64), bf16),
            pltpu.VMEM((2, 64, 128), f32),
            pltpu.VMEM((64, 256), bf16),
            pltpu.VMEM((65 * rows, 128), f32),
            pltpu.VMEM((64, 128 * rows), bf16),
            pltpu.VMEM((65 * rows, 128), f32),
            pltpu.VMEM((BATCHES, 64, rows // BATCHES, 128), bf16),
            pltpu.SemaphoreType.DMA((BATCHES, X_CUTS)),
            pltpu.SemaphoreType.DMA((6,)),
            pltpu.SemaphoreType.DMA((BATCHES,)),
        ],
        compiler_params=pltpu.CompilerParams(vmem_limit_bytes=16 * MIB),
        cost_estimate=pl.CostEstimate(flops=300_000_000, bytes_accessed=2 * MIB, transcendentals=0),
        name="contrib",
    )(*in_hbm(x, u, v, w, jnp.asarray(first), jnp.asarray(turn), jnp.asarray(last)))


def taper_kernel(sc_ref, own_ref, other_ref, trail_hbm, lead_hbm, b_ref, a_ref, trail_ref, lead_ref, sem):
    trail_copies = [
        pltpu.make_async_copy(trail_hbm.at[w], trail_ref.at[w], sem.at[w]) for w in range(NW)
    ]
    lead_copies = [
        pltpu.make_async_copy(lead_hbm.at[sc_ref[2], w], lead_ref.at[w], sem.at[NW + w]) for w in range(NW)
    ]
    for copy in trail_copies + lead_copies:
        copy.start()
    v_all = jnp.concatenate([own_ref[VT : 2 * VT, :], other_ref[VT : 2 * VT, :]], axis=0)
    u_all = jnp.concatenate([own_ref[0:VT, :], other_ref[0:VT, :]], axis=0)
    weights = jnp.concatenate(
        [own_ref[2 * VT : 2 * VT + 16, 0:VT], other_ref[2 * VT : 2 * VT + 16, 0:VT]], axis=1
    ).astype(f32)
    for w in range(NW):
        trail_copies[w].wait()
        re_at = slice(w * 256, (w + 1) * 256)
        im_at = slice(512 + w * 256, 512 + (w + 1) * 256)
        for j in range(FGRID):
            got = dot_nt(trail_ref[w, j * 128 : (j + 1) * 128, :], v_all)
            b_ref[j * 128 : (j + 1) * 128, re_at] = got.astype(bf16)
            b_ref[j * 128 : j * 128 + 64, im_at] = (-got[64:128]).astype(bf16)
            b_ref[j * 128 + 64 : (j + 1) * 128, im_at] = got[0:64].astype(bf16)
    for w in range(NW):
        lead_copies[w].wait()
        re_at = slice(w * 256, (w + 1) * 256)
        scale = weights[w : w + 1, :]
        a_ref[0, :, re_at] = (dot_nt(lead_ref[w, 0:256, :], u_all) * scale).astype(bf16)
        a_ref[1, :, re_at] = (dot_nt(lead_ref[w, 256:512, :], u_all) * scale).astype(bf16)


def taper_transforms(where, own, other):
    trailing, leading = taper_tables()
    anywhere = pl.BlockSpec(memory_space=pl.ANY)
    vmem = pl.BlockSpec(memory_space=pltpu.VMEM)
    return pl.pallas_call(
        taper_kernel,
        out_shape=(
            pltpu.VMEM((2 * SG, 1024), bf16),
            pltpu.VMEM((2, SG // 2, 512), bf16),
        ),
        in_specs=[pl.BlockSpec(memory_space=pltpu.SMEM), vmem, vmem, anywhere, anywhere],
        out_specs=(vmem, vmem),
        scratch_shapes=[
            pltpu.VMEM((NW, 2 * SG, SG), bf16),
            pltpu.VMEM((NW, SG, SG), bf16),
            pltpu.SemaphoreType.DMA((2 * NW,)),
        ],
        compiler_params=pltpu.CompilerParams(vmem_limit_bytes=24 * MIB),
        cost_estimate=pl.CostEstimate(flops=800_000_000, bytes_accessed=8 * MIB, transcendentals=0),
        name="tapers",
    )(where, own, other, *in_hbm(jnp.asarray(trailing), jnp.asarray(leading)))


def slots_kernel(sc_ref, table_ref, obs_ref, links_ref, gains_ref, out_ref, window, factors, link_sem, gain_sem):
    tiles = links_ref.shape[1] // 128
    begin = jnp.int32(0)
    blocks = []
    copies = []
    for b in range(NBLK):
        channel = table_ref[0, b]
        offset = table_ref[1, b]
        amount = table_ref[2, b]
        tile = jnp.minimum(offset // 128, tiles - LINK_WINDOW // 128)
        at = pl.multiple_of(tile * 128, 128)
        copies.append(
            pltpu.make_async_copy(links_ref.at[:, pl.ds(at, LINK_WINDOW)], window.at[b], link_sem.at[b])
        )
        copies.append(pltpu.make_async_copy(gains_ref.at[channel], factors.at[b], gain_sem.at[b]))
        blocks.append((channel, offset - at, amount, begin))
        begin = begin + amount
    for copy in copies:
        copy.start()
    slot = lax.broadcasted_iota(jnp.int32, (1, VT), 1)
    members = []
    chooser = []
    blocks_of = jnp.full((1, VT), -1.0, f32)
    channels = jnp.zeros((1, VT), f32)
    index = lax.broadcasted_iota(jnp.int32, (LINK_WINDOW, VT), 0)
    for b, (channel, shift, amount, start) in enumerate(blocks):
        inside = (slot >= start) & (slot < start + amount)
        member = jnp.where(inside, 1.0, 0.0)
        members.append(member)
        blocks_of = jnp.where(inside, float(b), blocks_of)
        channels = jnp.where(slot == NBLK * sc_ref[2] + (64 + b), channel.astype(f32), channels)
        want = jnp.where(inside, slot - start + shift, -1)
        chooser.append(jnp.where(index == want, 1.0, 0.0).astype(bf16))
    for copy in copies:
        copy.wait()
    digits = []
    for b in range(NBLK):
        found = window[b]
        high = found >> 4
        digits.append(jnp.concatenate([high, found - (high << 4)], axis=0).astype(f32).astype(bf16))
    picked = jnp.dot(
        jnp.concatenate(digits, axis=1), jnp.concatenate(chooser, axis=0), preferred_element_type=f32
    )
    stations = picked[0:2] * 16.0 + picked[2:4]
    both = jnp.concatenate([stations[0:1], stations[1:2]], axis=1).astype(jnp.int32)
    station_index = lax.broadcasted_iota(jnp.int32, (NST, 2 * VT), 0)
    onehot = jnp.where(station_index == both, 1.0, 0.0).astype(bf16)
    rest = jnp.concatenate([factors[b] for b in range(NBLK)], axis=0)
    taken = jnp.zeros((4 * NBLK, 2 * VT), f32)
    for piece in range(3):
        rounded = rest.astype(bf16)
        taken = taken + jnp.dot(rounded, onehot, preferred_element_type=f32)
        rest = rest - rounded.astype(f32)
    gain_first = jnp.zeros((4, VT), f32)
    gain_second = jnp.zeros((4, VT), f32)
    for b in range(NBLK):
        gain_first = gain_first + members[b] * taken[4 * b : 4 * b + 4, 0:VT]
        gain_second = gain_second + members[b] * taken[4 * b : 4 * b + 4, VT : 2 * VT]
    quarter = obs_ref.shape[3]
    lane = lax.broadcasted_iota(jnp.int32, (1, VT), 1)
    mine = (lane // quarter) == sc_ref[1]
    out_ref[0:1, :] = jnp.full((1, VT), sc_ref[2].astype(f32))
    out_ref[1:2, :] = jnp.full((1, VT), sc_ref[1].astype(f32))
    out_ref[2:4, :] = jnp.zeros((2, VT), f32)
    for row in range(2 * NPOL):
        one = obs_ref[0, row]
        spread = jnp.concatenate([one] * (VT // quarter), axis=1)
        out_ref[4 + row : 5 + row, :] = jnp.where(mine, spread, 0.0)
    out_ref[12:16, :] = gain_first
    out_ref[16:20, :] = gain_second
    out_ref[20:22, :] = stations
    out_ref[22:23, :] = blocks_of
    out_ref[23:24, :] = channels


def slot_rows(where, table, observed, links, gains):
    smem = pl.BlockSpec(memory_space=pltpu.SMEM)
    anywhere = pl.BlockSpec(memory_space=pl.ANY)
    return pl.pallas_call(
        slots_kernel,
        out_shape=jax.ShapeDtypeStruct((24, VT), f32),
        in_specs=[smem, smem, pl.BlockSpec(memory_space=pltpu.VMEM), anywhere, anywhere],
        out_specs=pl.BlockSpec(memory_space=pltpu.VMEM),
        scratch_shapes=[
            pltpu.VMEM((NBLK, 2, LINK_WINDOW), jnp.int32),
            pltpu.VMEM((NBLK, 4, NST), f32),
            pltpu.SemaphoreType.DMA((NBLK,)),
            pltpu.SemaphoreType.DMA((NBLK,)),
        ],
        compiler_params=pltpu.CompilerParams(vmem_limit_bytes=8 * MIB),
        cost_estimate=pl.CostEstimate(flops=50_000_000, bytes_accessed=2 * MIB, transcendentals=0),
        name="slots",
    )(where, table, observed, *in_hbm(links, gains))


def predict_kernel(got_ref, b_ref, a_ref, info_ref, out_ref):
    rows = got_ref.shape[1]
    left = jnp.concatenate(
        [
            jnp.concatenate([got_ref[i * FGRID + j] for j in range(FGRID)], axis=1)
            for i in range(FGRID)
        ],
        axis=0,
    )
    del rows
    total_re = [jnp.zeros((1, VT), f32), jnp.zeros((1, VT), f32)]
    total_im = [jnp.zeros((1, VT), f32), jnp.zeros((1, VT), f32)]
    for w in range(NW):
        at = slice(w * 256, (w + 1) * 256)
        along_re = jnp.dot(left, b_ref[:, w * 256 : (w + 1) * 256], preferred_element_type=f32)
        along_im = jnp.dot(left, b_ref[:, 512 + w * 256 : 512 + (w + 1) * 256], preferred_element_type=f32)
        a_re = a_ref[0, :, at].astype(f32)
        a_im = a_ref[1, :, at].astype(f32)
        sum_re = jnp.sum(a_re * along_re - a_im * along_im, axis=0, keepdims=True)
        sum_im = jnp.sum(a_re * along_im + a_im * along_re, axis=0, keepdims=True)
        for side in range(2):
            total_re[side] = total_re[side] + sum_re[:, side * VT : (side + 1) * VT]
            total_im[side] = total_im[side] + sum_im[:, side * VT : (side + 1) * VT]
    first = info_ref[0:1, :] == 0.0
    rows_out = [
        jnp.where(first, total_re[0], total_re[1]),
        jnp.where(first, total_re[1], total_re[0]),
        jnp.where(first, total_im[0], total_im[1]),
        jnp.where(first, total_im[1], total_im[0]),
    ]
    head = jnp.concatenate(rows_out + [info_ref[4:8, :]], axis=0)
    for to in range(out_ref.shape[0]):
        out_ref[to, 0:8, :] = head
        out_ref[to, 8:24, :] = info_ref[8:24, :]


def partial_predictions(got, b, a, info, peers):
    vmem = pl.BlockSpec(memory_space=pltpu.VMEM)
    return pl.pallas_call(
        predict_kernel,
        out_shape=jax.ShapeDtypeStruct((peers, 24, VT), f32),
        in_specs=[vmem] * 4,
        out_specs=vmem,
        compiler_params=pltpu.CompilerParams(vmem_limit_bytes=20 * MIB),
        cost_estimate=pl.CostEstimate(flops=540_000_000, bytes_accessed=4 * MIB, transcendentals=0),
        name="predict",
    )(got, b, a, info)


def gradient_kernel(info_ref, got_ref, resid_ref, out_ref):
    owners = 2
    own_tm = info_ref[0:1, :]
    own_pol = info_ref[1:2, :]
    own_class = (own_pol * owners + own_tm).astype(jnp.int32)
    row_id = lax.broadcasted_iota(jnp.int32, (NST // 8, VT), 0)
    block_row = lax.broadcasted_iota(jnp.int32, (VT, VT), 0) >> 2
    channels = got_ref[0, 23:24, :] + got_ref[1, 23:24, :]
    pick = lambda rows, order: jnp.concatenate([rows[i : i + 1] for i in order], axis=0)
    masks = {}
    values = {}
    resid_owner = []
    for o in range(owners):
        info = got_ref[o]
        measured = got_ref[o, 4:12, :]
        for p in range(1, NPOL):
            measured = measured + got_ref[p * owners + o, 4:12, :]
        pred_re = []
        pred_im = []
        for p in range(NPOL):
            one, two = got_ref[p * owners], got_ref[p * owners + 1]
            pred_re.append(one[o : o + 1] + two[o : o + 1])
            pred_im.append(one[2 + o : 3 + o] + two[2 + o : 3 + o])
        pred_re = jnp.concatenate(pred_re, axis=0)
        pred_im = jnp.concatenate(pred_im, axis=0)
        gain_first = info[12:16]
        gain_second = info[16:20]
        block = info[22:23].astype(jnp.int32)
        live = jnp.where(block >= 0, 1.0, 0.0)
        first_re = pick(gain_first, (0, 0, 2, 2))
        first_im = pick(gain_first, (1, 1, 3, 3))
        second_re = pick(gain_second, (0, 2, 0, 2))
        second_im = pick(gain_second, (1, 3, 1, 3))
        obs_re = pick(measured, (0, 2, 4, 6))
        obs_im = pick(measured, (1, 3, 5, 7))
        both_re = first_re * second_re + first_im * second_im
        both_im = first_im * second_re - first_re * second_im
        resid_re = live * (obs_re - (both_re * pred_re - both_im * pred_im))
        resid_im = live * (obs_im - (both_re * pred_im + both_im * pred_re))
        cross_re = second_re * pred_re + second_im * pred_im
        cross_im = second_im * pred_re - second_re * pred_im
        lead_re = -(resid_re * cross_re - resid_im * cross_im)
        lead_im = -(resid_re * cross_im + resid_im * cross_re)
        along_re = first_re * pred_re - first_im * pred_im
        along_im = first_re * pred_im + first_im * pred_re
        trail_re = -(resid_re * along_re + resid_im * along_im)
        trail_im = -(resid_re * along_im - resid_im * along_re)
        leading = jnp.concatenate(
            [
                lead_re[0:1] + lead_re[1:2],
                lead_im[0:1] + lead_im[1:2],
                lead_re[2:3] + lead_re[3:4],
                lead_im[2:3] + lead_im[3:4],
            ],
            axis=0,
        )
        trailing = jnp.concatenate(
            [
                trail_re[0:1] + trail_re[2:3],
                trail_im[0:1] + trail_im[2:3],
                trail_re[1:2] + trail_re[3:4],
                trail_im[1:2] + trail_im[3:4],
            ],
            axis=0,
        )
        resid_owner.append(
            jnp.concatenate(
                [r for p in range(NPOL) for r in (resid_re[p : p + 1], resid_im[p : p + 1])], axis=0
            )
        )
        chosen = block_row == jnp.where(block >= 0, NBLK * o + block, -1)
        for side, terms in ((0, leading), (1, trailing)):
            station = info[20 + side : 21 + side].astype(jnp.int32)
            key = jnp.where((station & 7) == own_class, station >> 3, -1)
            masks[side, o] = jnp.where(row_id == key, 1.0, 0.0).astype(bf16)
            tall = jnp.concatenate([terms, terms], axis=0)
            tall = jnp.concatenate([tall] * 16, axis=0)
            values[side, o] = jnp.where(chosen, tall, 0.0).astype(bf16)
    order = [(side, o) for side in range(2) for o in range(owners)]
    mask = jnp.concatenate([masks[at] for at in order], axis=1)
    value = jnp.concatenate([values[at] for at in order], axis=1)
    out_ref[...] = dot_nt(mask, value) + channels
    mine = jnp.where(own_tm == 0.0, resid_owner[0], resid_owner[1])
    quarter = resid_ref.shape[1]
    part = mine[:, 0:quarter]
    for q in range(1, NPOL):
        part = jnp.where(own_pol[:, 0:quarter] == float(q), mine[:, q * quarter : (q + 1) * quarter], part)
    resid_ref[...] = part


def gradient_rows(info, got):
    vmem = pl.BlockSpec(memory_space=pltpu.VMEM)
    return pl.pallas_call(
        gradient_kernel,
        out_shape=(
            pltpu.VMEM((2 * NPOL, VT // NPOL), f32),
            pltpu.VMEM((NST // 8, 128), f32),
        ),
        in_specs=[vmem, vmem],
        out_specs=(vmem, vmem),
        compiler_params=pltpu.CompilerParams(vmem_limit_bytes=12 * MIB),
        cost_estimate=pl.CostEstimate(flops=70_000_000, bytes_accessed=MIB, transcendentals=0),
        name="gradient",
    )(info, got)


def collect_kernel(got_ref, mine_ref, out_hbm, resid_hbm, out_ref, resid_ref, sem):
    part = mine_ref[...]
    for row in range(2 * NPOL):
        resid_ref[0, row] = part[row : row + 1, :]
    resid_copy = pltpu.make_async_copy(resid_ref, resid_hbm, sem.at[0])
    resid_copy.start()
    turned = got_ref[...].T
    lanes = turned.shape[1]
    channel_row = lax.broadcasted_iota(jnp.int32, (128, lanes), 0) >> 2
    group_row = lax.broadcasted_iota(jnp.int32, (8, lanes), 0)
    values = []
    groups = []
    for block in range(2 * NBLK):
        channel = turned[64 + block : 65 + block].astype(jnp.int32)
        terms = turned[4 * block : 4 * block + 4]
        tall = jnp.concatenate([terms, terms], axis=0)
        tall = jnp.concatenate([tall] * 16, axis=0)
        value = jnp.where(channel_row == (channel & 31), tall, 0.0).astype(bf16)
        group = jnp.where(group_row == (channel >> 5), 1.0, 0.0).astype(bf16)
        values.append(value)
        groups.append(group)
    total = dot_nt(jnp.concatenate(groups, axis=1), jnp.concatenate(values, axis=1))
    out_ref[...] = grad_scale * total
    out_copy = pltpu.make_async_copy(out_ref, out_hbm, sem.at[1])
    out_copy.start()
    out_copy.wait()
    resid_copy.wait()


def collect_rows(got, mine, quarter):
    vmem = pl.BlockSpec(memory_space=pltpu.VMEM)
    return pl.pallas_call(
        collect_kernel,
        out_shape=(
            jax.ShapeDtypeStruct((8, 128), f32),
            jax.ShapeDtypeStruct((1, 2 * NPOL, 1, quarter), f32),
        ),
        in_specs=[vmem, vmem],
        out_specs=(pl.BlockSpec(memory_space=pl.ANY),) * 2,
        scratch_shapes=[
            pltpu.VMEM((8, 128), f32),
            pltpu.VMEM((1, 2 * NPOL, 1, quarter), f32),
            pltpu.SemaphoreType.DMA((2,)),
        ],
        compiler_params=pltpu.CompilerParams(vmem_limit_bytes=8 * MIB),
        cost_estimate=pl.CostEstimate(flops=2_000_000, bytes_accessed=65536, transcendentals=0),
        name="collect",
    )(got, mine)


def on_device(
    tile_spectral_lines,
    taper_leading_axis,
    taper_trailing_axis,
    depth_layer_factors,
    measured_correlations,
    visibility_groups_table,
    antenna_links,
    complex_receiver_factors,
):
    where = jnp.stack([lax.axis_index("facet"), lax.axis_index("pol"), lax.axis_index("tm")]).astype(jnp.int32)
    quarter = measured_correlations.shape[3]
    u = taper_leading_axis.reshape(VT, SG)
    v = taper_trailing_axis.reshape(VT, SG)
    w = depth_layer_factors.reshape(NW, VT)
    x = tile_spectral_lines.reshape(tile_spectral_lines.shape[2:])
    contrib, pack = contributions(x, u, v, w)
    received = lax.all_to_all(contrib, "facet", split_axis=0, concat_axis=0, tiled=True)
    other = lax.ppermute(pack, "tm", [(0, 1), (1, 0)])
    b, a = taper_transforms(where, pack, other)
    info = slot_rows(
        where,
        visibility_groups_table.reshape(3, NBLK),
        measured_correlations,
        antenna_links,
        complex_receiver_factors,
    )
    peers = lax.axis_size(("pol", "tm"))
    sent = partial_predictions(received, b, a, info, peers)
    gathered = lax.all_to_all(sent, ("pol", "tm"), split_axis=0, concat_axis=0, tiled=True)
    mine, partial_rows = gradient_rows(info, gathered)
    rows = lax.all_to_all(
        partial_rows.reshape(NST // 8, 1, 128), "facet", split_axis=0, concat_axis=0, tiled=True
    )
    gain_grad, residual = collect_rows(rows.reshape(NST // 8, 128), mine, quarter)
    return (residual, gain_grad.reshape(1, 4 * NCH))


def solution(mesh):
    return jax.shard_map(
        on_device,
        mesh=mesh,
        in_specs=(
            P("facet", "pol", None, "tm", None),
            P("facet", "tm", None, None),
            P("facet", "tm", None, None),
            P("facet", "tm", None, None),
            P("facet", None, "tm", "pol"),
            P("facet", "tm", None, None),
            P(),
            P(),
        ),
        out_specs=(P("facet", None, "tm", "pol"), P(("facet", "pol", "tm"), None)),
        check_vma=False,
    )
```

```python
import functools
import math

import jax
import jax.numpy as jnp
import ml_dtypes
import numpy as np
from jax import lax
from jax.experimental import pallas as pl
from jax.experimental.pallas import tpu as pltpu
from jax.sharding import PartitionSpec as P

FGRID = 8
FS = 4096
MC = 64
SG = 512
NPOL = 4
NW = 2
NCH = 256
NST = 512
VT = 128
NBLK = 8
LINK_WINDOW = 256
BATCHES = 2
X_CUTS = 4

w_chirp = 0.37
grad_scale = 0.1
MIB = 1 << 20

bf16 = jnp.bfloat16
f32 = jnp.float32
NT = (((1,), (1,)), ((), ()))


def dot_nt(left, right):
    return lax.dot_general(left, right, NT, preferred_element_type=f32)


def np_bf16(table):
    return np.asarray(table, np.float64).astype(np.float32).astype(ml_dtypes.bfloat16)


@functools.cache
def section_tables():
    a = np.arange(32)
    angle = -2 * np.pi * ((a[:, None] * a[None, :]) % 32) / 32
    c, s = np.cos(angle), np.sin(angle)
    first = np.block([[c, -s], [s, c]])
    k = np.arange(64)[:, None]
    l = np.arange(128)[None, :]
    turn = -2 * np.pi * ((k * l) % FS) / FS
    sub = np.arange(64)[:, None]
    angle = -2 * np.pi * ((sub * l) % 64) / 64
    last = np.concatenate([np.cos(angle), np.sin(angle)], axis=1) / math.sqrt(FS)
    return (
        np_bf16(first),
        np.stack([np.cos(turn), np.sin(turn)]).astype(np.float32),
        np_bf16(last),
    )


@functools.cache
def taper_tables():
    x = np.arange(SG)
    angle = 2 * np.pi * ((x[:, None] * x[None, :]) % SG) / SG
    table = np.exp(1j * angle) / math.sqrt(SG)
    across = (x - SG // 2) ** 2 * (w_chirp / SG**2)
    trailing, leading = [], []
    for w in range(NW):
        full = table * np.exp(2j * np.pi * w * across)[None, :]
        rows = np.stack([full.real, -full.imag]).reshape(2, FGRID, MC, SG)
        trailing.append(rows.transpose(1, 0, 2, 3).reshape(2 * SG, SG))
        halves = np.stack([full.real, full.imag]).reshape(2, FGRID, 2, MC // 2, SG)
        leading.append(halves.transpose(2, 0, 1, 3, 4).reshape(2, 2 * SG // 2, SG))
    return np_bf16(np.stack(trailing)), np_bf16(np.stack(leading, axis=1))


def in_hbm(*arrays):
    return [pltpu.with_memory_space_constraint(one, pltpu.HBM) for one in arrays]


def contrib_kernel(
    x_hbm, u_hbm, v_hbm, w_hbm, first_hbm, turn_hbm, last_hbm,
    out_hbm, pack_ref,
    x_ref, w_ref, first_ref, turn_ref, last_ref, spread, lined, placed, out_ref, x_sem, sem, out_sem,
):
    rows = x_ref.shape[1]
    batch = rows // BATCHES
    wide = FS // X_CUTS
    pieces = [
        pltpu.make_async_copy(
            x_hbm.at[:, pl.ds(h * batch, batch), pl.ds(c * wide, wide)],
            x_ref.at[:, pl.ds(h * batch, batch), pl.ds(c * wide, wide)],
            x_sem.at[h, c],
        )
        for h in range(BATCHES)
        for c in range(X_CUTS)
    ]
    tables = [
        pltpu.make_async_copy(source, target, sem.at[i])
        for i, (source, target) in enumerate(
            ((first_hbm, first_ref), (turn_hbm, turn_ref), (last_hbm, last_ref))
        )
    ]
    tapers = [
        pltpu.make_async_copy(source, target, sem.at[3 + i])
        for i, (source, target) in enumerate(
            (
                (w_hbm, w_ref),
                (u_hbm, pack_ref.at[pl.ds(0, VT), :]),
                (v_hbm, pack_ref.at[pl.ds(VT, VT), :]),
            )
        )
    ]
    results = [
        pltpu.make_async_copy(out_ref.at[h], out_hbm.at[:, pl.ds(h * batch, batch), :], out_sem.at[h])
        for h in range(BATCHES)
    ]
    for copy in pieces[:X_CUTS] + tables + pieces[X_CUTS:]:
        copy.start()

    def section_of(pair):
        return jnp.dot(first_ref[...], lined[:, pair * 256 : (pair + 1) * 256], preferred_element_type=f32)

    def turned_of(section):
        turn_re = turn_ref[0]
        turn_im = turn_ref[1]
        sides = []
        for half in range(2):
            one = section[:, half * 128 : (half + 1) * 128]
            re = jnp.concatenate([one[0:32], one[0:32]], axis=0)
            im = jnp.concatenate([one[32:64], one[32:64]], axis=0)
            turned_re = (re * turn_re - im * turn_im).astype(bf16)
            turned_im = (re * turn_im + im * turn_re).astype(bf16)
            sides.append(
                jnp.concatenate(
                    [
                        jnp.concatenate([turned_re, -turned_im], axis=1),
                        jnp.concatenate([turned_im, turned_re], axis=1),
                    ],
                    axis=0,
                )
            )
        return jnp.concatenate(sides, axis=0)

    def finish(pair, turned):
        result = dot_nt(last_ref[...], turned)
        placed[pl.ds(2 * pair, 64, stride=rows), :] = result[:, 0:128]
        placed[pl.ds(2 * pair + 1, 64, stride=rows), :] = result[:, 128:256]

    def line_up(h):
        for c in range(X_CUTS):
            pieces[h * X_CUTS + c].wait()
            take(h, c)
        for m in range(h * batch, (h + 1) * batch):
            lined[:, m * 128 : (m + 1) * 128] = spread[pl.ds(m, 64, stride=rows), :].astype(bf16)

    def take(h, c):
        for part in range(2):
            for a in range(c * 32 // X_CUTS, (c + 1) * 32 // X_CUTS):
                at = (part * 32 + a) * rows + h * batch
                spread[at : at + batch, :] = x_ref[
                    part, h * batch : (h + 1) * batch, a * 128 : (a + 1) * 128
                ].astype(f32)

    def send(h):
        for s in range(64):
            at = s * rows + h * batch
            out_ref[h, s] = placed[at : at + batch, :].astype(bf16)
        results[h].start()

    per = batch // 2
    line_up(0)
    for copy in tapers:
        copy.start()
    for copy in tables:
        copy.wait()
    pairs = rows // 2
    sections = {0: section_of(0), 1: section_of(1)}
    turned = {}
    for step in range(pairs + 1):
        if step + 2 < pairs:
            if (step + 2) % per == 0:
                line_up((step + 2) // per)
            sections[step + 2] = section_of(step + 2)
        if step < pairs:
            turned[step] = turned_of(sections.pop(step))
        if step >= 1:
            finish(step - 1, turned.pop(step - 1))
            if step % per == 0:
                send(step // per - 1)
    for copy in tapers:
        copy.wait()
    weights = jnp.concatenate([w_ref[...].astype(f32), jnp.zeros((16 - NW, VT), f32)], axis=0).astype(bf16)
    pack_ref[2 * VT : 2 * VT + 16, :] = jnp.concatenate([weights] * (SG // VT), axis=1)
    for copy in results:
        copy.wait()


def contributions(x, u, v, w):
    rows = x.shape[1]
    first, turn, last = section_tables()
    anywhere = pl.BlockSpec(memory_space=pl.ANY)
    vmem = pl.BlockSpec(memory_space=pltpu.VMEM)
    return pl.pallas_call(
        contrib_kernel,
        out_shape=(
            jax.ShapeDtypeStruct((64, rows, 128), bf16),
            pltpu.VMEM((2 * VT + 16, SG), bf16),
        ),
        in_specs=[anywhere] * 7,
        out_specs=(anywhere, vmem),
        scratch_shapes=[
            pltpu.VMEM((2, rows, FS), bf16),
            pltpu.VMEM((NW, VT), bf16),
            pltpu.VMEM((64, 64), bf16),
            pltpu.VMEM((2, 64, 128), f32),
            pltpu.VMEM((64, 256), bf16),
            pltpu.VMEM((65 * rows, 128), f32),
            pltpu.VMEM((64, 128 * rows), bf16),
            pltpu.VMEM((65 * rows, 128), f32),
            pltpu.VMEM((BATCHES, 64, rows // BATCHES, 128), bf16),
            pltpu.SemaphoreType.DMA((BATCHES, X_CUTS)),
            pltpu.SemaphoreType.DMA((6,)),
            pltpu.SemaphoreType.DMA((BATCHES,)),
        ],
        compiler_params=pltpu.CompilerParams(vmem_limit_bytes=16 * MIB),
        cost_estimate=pl.CostEstimate(flops=300_000_000, bytes_accessed=2 * MIB, transcendentals=0),
        name="contrib",
    )(*in_hbm(x, u, v, w, jnp.asarray(first), jnp.asarray(turn), jnp.asarray(last)))


def taper_kernel(sc_ref, own_ref, other_ref, trail_hbm, lead_hbm, b_ref, a_ref, trail_ref, lead_ref, sem):
    trail_copies = [
        pltpu.make_async_copy(trail_hbm.at[w], trail_ref.at[w], sem.at[w]) for w in range(NW)
    ]
    lead_copies = [
        pltpu.make_async_copy(lead_hbm.at[sc_ref[2], w], lead_ref.at[w], sem.at[NW + w]) for w in range(NW)
    ]
    for copy in trail_copies + lead_copies:
        copy.start()
    v_all = jnp.concatenate([own_ref[VT : 2 * VT, :], other_ref[VT : 2 * VT, :]], axis=0)
    u_all = jnp.concatenate([own_ref[0:VT, :], other_ref[0:VT, :]], axis=0)
    weights = jnp.concatenate(
        [own_ref[2 * VT : 2 * VT + 16, 0:VT], other_ref[2 * VT : 2 * VT + 16, 0:VT]], axis=1
    ).astype(f32)
    for w in range(NW):
        trail_copies[w].wait()
        re_at = slice(w * 256, (w + 1) * 256)
        im_at = slice(512 + w * 256, 512 + (w + 1) * 256)
        for j in range(FGRID):
            got = dot_nt(trail_ref[w, j * 128 : (j + 1) * 128, :], v_all)
            b_ref[j * 128 : (j + 1) * 128, re_at] = got.astype(bf16)
            b_ref[j * 128 : j * 128 + 64, im_at] = (-got[64:128]).astype(bf16)
            b_ref[j * 128 + 64 : (j + 1) * 128, im_at] = got[0:64].astype(bf16)
    for w in range(NW):
        lead_copies[w].wait()
        re_at = slice(w * 256, (w + 1) * 256)
        scale = weights[w : w + 1, :]
        a_ref[0, :, re_at] = (dot_nt(lead_ref[w, 0:256, :], u_all) * scale).astype(bf16)
        a_ref[1, :, re_at] = (dot_nt(lead_ref[w, 256:512, :], u_all) * scale).astype(bf16)


def taper_transforms(where, own, other):
    trailing, leading = taper_tables()
    anywhere = pl.BlockSpec(memory_space=pl.ANY)
    vmem = pl.BlockSpec(memory_space=pltpu.VMEM)
    return pl.pallas_call(
        taper_kernel,
        out_shape=(
            pltpu.VMEM((2 * SG, 1024), bf16),
            pltpu.VMEM((2, SG // 2, 512), bf16),
        ),
        in_specs=[pl.BlockSpec(memory_space=pltpu.SMEM), vmem, vmem, anywhere, anywhere],
        out_specs=(vmem, vmem),
        scratch_shapes=[
            pltpu.VMEM((NW, 2 * SG, SG), bf16),
            pltpu.VMEM((NW, SG, SG), bf16),
            pltpu.SemaphoreType.DMA((2 * NW,)),
        ],
        compiler_params=pltpu.CompilerParams(vmem_limit_bytes=24 * MIB),
        cost_estimate=pl.CostEstimate(flops=800_000_000, bytes_accessed=8 * MIB, transcendentals=0),
        name="tapers",
    )(where, own, other, *in_hbm(jnp.asarray(trailing), jnp.asarray(leading)))


def slots_kernel(sc_ref, table_ref, obs_ref, links_ref, gains_ref, out_ref, window, factors, link_sem, gain_sem):
    tiles = links_ref.shape[1] // 128
    begin = jnp.int32(0)
    blocks = []
    copies = []
    for b in range(NBLK):
        channel = table_ref[0, b]
        offset = table_ref[1, b]
        amount = table_ref[2, b]
        tile = jnp.minimum(offset // 128, tiles - LINK_WINDOW // 128)
        at = pl.multiple_of(tile * 128, 128)
        copies.append(
            pltpu.make_async_copy(links_ref.at[:, pl.ds(at, LINK_WINDOW)], window.at[b], link_sem.at[b])
        )
        copies.append(pltpu.make_async_copy(gains_ref.at[channel], factors.at[b], gain_sem.at[b]))
        blocks.append((channel, offset - at, amount, begin))
        begin = begin + amount
    for copy in copies:
        copy.start()
    slot = lax.broadcasted_iota(jnp.int32, (1, VT), 1)
    members = []
    chooser = []
    blocks_of = jnp.full((1, VT), -1.0, f32)
    channels = jnp.zeros((1, VT), f32)
    index = lax.broadcasted_iota(jnp.int32, (LINK_WINDOW, VT), 0)
    for b, (channel, shift, amount, start) in enumerate(blocks):
        inside = (slot >= start) & (slot < start + amount)
        member = jnp.where(inside, 1.0, 0.0)
        members.append(member)
        blocks_of = jnp.where(inside, float(b), blocks_of)
        channels = jnp.where(slot == NBLK * sc_ref[2] + (64 + b), channel.astype(f32), channels)
        want = jnp.where(inside, slot - start + shift, -1)
        chooser.append(jnp.where(index == want, 1.0, 0.0).astype(bf16))
    for copy in copies:
        copy.wait()
    digits = []
    for b in range(NBLK):
        found = window[b]
        high = found >> 4
        digits.append(jnp.concatenate([high, found - (high << 4)], axis=0).astype(f32).astype(bf16))
    picked = jnp.dot(
        jnp.concatenate(digits, axis=1), jnp.concatenate(chooser, axis=0), preferred_element_type=f32
    )
    stations = picked[0:2] * 16.0 + picked[2:4]
    both = jnp.concatenate([stations[0:1], stations[1:2]], axis=1).astype(jnp.int32)
    station_index = lax.broadcasted_iota(jnp.int32, (NST, 2 * VT), 0)
    onehot = jnp.where(station_index == both, 1.0, 0.0).astype(bf16)
    rest = jnp.concatenate([factors[b] for b in range(NBLK)], axis=0)
    taken = jnp.zeros((4 * NBLK, 2 * VT), f32)
    for piece in range(3):
        rounded = rest.astype(bf16)
        taken = taken + jnp.dot(rounded, onehot, preferred_element_type=f32)
        rest = rest - rounded.astype(f32)
    gain_first = jnp.zeros((4, VT), f32)
    gain_second = jnp.zeros((4, VT), f32)
    for b in range(NBLK):
        gain_first = gain_first + members[b] * taken[4 * b : 4 * b + 4, 0:VT]
        gain_second = gain_second + members[b] * taken[4 * b : 4 * b + 4, VT : 2 * VT]
    quarter = obs_ref.shape[3]
    lane = lax.broadcasted_iota(jnp.int32, (1, VT), 1)
    mine = (lane // quarter) == sc_ref[1]
    out_ref[0:1, :] = jnp.full((1, VT), sc_ref[2].astype(f32))
    out_ref[1:2, :] = jnp.full((1, VT), sc_ref[1].astype(f32))
    out_ref[2:4, :] = jnp.zeros((2, VT), f32)
    for row in range(2 * NPOL):
        one = obs_ref[0, row]
        spread = jnp.concatenate([one] * (VT // quarter), axis=1)
        out_ref[4 + row : 5 + row, :] = jnp.where(mine, spread, 0.0)
    out_ref[12:16, :] = gain_first
    out_ref[16:20, :] = gain_second
    out_ref[20:22, :] = stations
    out_ref[22:23, :] = blocks_of
    out_ref[23:24, :] = channels


def slot_rows(where, table, observed, links, gains):
    smem = pl.BlockSpec(memory_space=pltpu.SMEM)
    anywhere = pl.BlockSpec(memory_space=pl.ANY)
    return pl.pallas_call(
        slots_kernel,
        out_shape=jax.ShapeDtypeStruct((24, VT), f32),
        in_specs=[smem, smem, pl.BlockSpec(memory_space=pltpu.VMEM), anywhere, anywhere],
        out_specs=pl.BlockSpec(memory_space=pltpu.VMEM),
        scratch_shapes=[
            pltpu.VMEM((NBLK, 2, LINK_WINDOW), jnp.int32),
            pltpu.VMEM((NBLK, 4, NST), f32),
            pltpu.SemaphoreType.DMA((NBLK,)),
            pltpu.SemaphoreType.DMA((NBLK,)),
        ],
        compiler_params=pltpu.CompilerParams(vmem_limit_bytes=8 * MIB),
        cost_estimate=pl.CostEstimate(flops=50_000_000, bytes_accessed=2 * MIB, transcendentals=0),
        name="slots",
    )(where, table, observed, *in_hbm(links, gains))


def predict_kernel(got_ref, b_ref, a_ref, info_ref, out_ref):
    rows = got_ref.shape[1]
    left = jnp.concatenate(
        [
            jnp.concatenate([got_ref[i * FGRID + j] for j in range(FGRID)], axis=1)
            for i in range(FGRID)
        ],
        axis=0,
    )
    del rows
    total_re = [jnp.zeros((1, VT), f32), jnp.zeros((1, VT), f32)]
    total_im = [jnp.zeros((1, VT), f32), jnp.zeros((1, VT), f32)]
    for w in range(NW):
        at = slice(w * 256, (w + 1) * 256)
        along_re = jnp.dot(left, b_ref[:, w * 256 : (w + 1) * 256], preferred_element_type=f32)
        along_im = jnp.dot(left, b_ref[:, 512 + w * 256 : 512 + (w + 1) * 256], preferred_element_type=f32)
        a_re = a_ref[0, :, at].astype(f32)
        a_im = a_ref[1, :, at].astype(f32)
        sum_re = jnp.sum(a_re * along_re - a_im * along_im, axis=0, keepdims=True)
        sum_im = jnp.sum(a_re * along_im + a_im * along_re, axis=0, keepdims=True)
        for side in range(2):
            total_re[side] = total_re[side] + sum_re[:, side * VT : (side + 1) * VT]
            total_im[side] = total_im[side] + sum_im[:, side * VT : (side + 1) * VT]
    first = info_ref[0:1, :] == 0.0
    rows_out = [
        jnp.where(first, total_re[0], total_re[1]),
        jnp.where(first, total_re[1], total_re[0]),
        jnp.where(first, total_im[0], total_im[1]),
        jnp.where(first, total_im[1], total_im[0]),
    ]
    head = jnp.concatenate(rows_out + [info_ref[4:8, :]], axis=0)
    for to in range(out_ref.shape[0]):
        out_ref[to, 0:8, :] = head
        out_ref[to, 8:24, :] = info_ref[8:24, :]


def partial_predictions(got, b, a, info, peers):
    vmem = pl.BlockSpec(memory_space=pltpu.VMEM)
    return pl.pallas_call(
        predict_kernel,
        out_shape=jax.ShapeDtypeStruct((peers, 24, VT), f32),
        in_specs=[vmem] * 4,
        out_specs=vmem,
        compiler_params=pltpu.CompilerParams(vmem_limit_bytes=20 * MIB),
        cost_estimate=pl.CostEstimate(flops=540_000_000, bytes_accessed=4 * MIB, transcendentals=0),
        name="predict",
    )(got, b, a, info)


def gradient_kernel(info_ref, got_ref, resid_ref, out_ref):
    owners = 2
    own_tm = info_ref[0:1, :]
    own_pol = info_ref[1:2, :]
    own_class = (own_pol * owners + own_tm).astype(jnp.int32)
    row_id = lax.broadcasted_iota(jnp.int32, (NST // 8, VT), 0)
    block_row = lax.broadcasted_iota(jnp.int32, (VT, VT), 0) >> 2
    channels = got_ref[0, 23:24, :] + got_ref[1, 23:24, :]
    pick = lambda rows, order: jnp.concatenate([rows[i : i + 1] for i in order], axis=0)
    masks = {}
    values = {}
    resid_owner = []
    for o in range(owners):
        info = got_ref[o]
        measured = got_ref[o, 4:12, :]
        for p in range(1, NPOL):
            measured = measured + got_ref[p * owners + o, 4:12, :]
        pred_re = []
        pred_im = []
        for p in range(NPOL):
            one, two = got_ref[p * owners], got_ref[p * owners + 1]
            pred_re.append(one[o : o + 1] + two[o : o + 1])
            pred_im.append(one[2 + o : 3 + o] + two[2 + o : 3 + o])
        pred_re = jnp.concatenate(pred_re, axis=0)
        pred_im = jnp.concatenate(pred_im, axis=0)
        gain_first = info[12:16]
        gain_second = info[16:20]
        block = info[22:23].astype(jnp.int32)
        live = jnp.where(block >= 0, 1.0, 0.0)
        first_re = pick(gain_first, (0, 0, 2, 2))
        first_im = pick(gain_first, (1, 1, 3, 3))
        second_re = pick(gain_second, (0, 2, 0, 2))
        second_im = pick(gain_second, (1, 3, 1, 3))
        obs_re = pick(measured, (0, 2, 4, 6))
        obs_im = pick(measured, (1, 3, 5, 7))
        both_re = first_re * second_re + first_im * second_im
        both_im = first_im * second_re - first_re * second_im
        resid_re = live * (obs_re - (both_re * pred_re - both_im * pred_im))
        resid_im = live * (obs_im - (both_re * pred_im + both_im * pred_re))
        cross_re = second_re * pred_re + second_im * pred_im
        cross_im = second_im * pred_re - second_re * pred_im
        lead_re = -(resid_re * cross_re - resid_im * cross_im)
        lead_im = -(resid_re * cross_im + resid_im * cross_re)
        along_re = first_re * pred_re - first_im * pred_im
        along_im = first_re * pred_im + first_im * pred_re
        trail_re = -(resid_re * along_re + resid_im * along_im)
        trail_im = -(resid_re * along_im - resid_im * along_re)
        leading = jnp.concatenate(
            [
                lead_re[0:1] + lead_re[1:2],
                lead_im[0:1] + lead_im[1:2],
                lead_re[2:3] + lead_re[3:4],
                lead_im[2:3] + lead_im[3:4],
            ],
            axis=0,
        )
        trailing = jnp.concatenate(
            [
                trail_re[0:1] + trail_re[2:3],
                trail_im[0:1] + trail_im[2:3],
                trail_re[1:2] + trail_re[3:4],
                trail_im[1:2] + trail_im[3:4],
            ],
            axis=0,
        )
        resid_owner.append(
            jnp.concatenate(
                [r for p in range(NPOL) for r in (resid_re[p : p + 1], resid_im[p : p + 1])], axis=0
            )
        )
        chosen = block_row == jnp.where(block >= 0, NBLK * o + block, -1)
        for side, terms in ((0, leading), (1, trailing)):
            station = info[20 + side : 21 + side].astype(jnp.int32)
            key = jnp.where((station & 7) == own_class, station >> 3, -1)
            masks[side, o] = jnp.where(row_id == key, 1.0, 0.0).astype(bf16)
            tall = jnp.concatenate([terms, terms], axis=0)
            tall = jnp.concatenate([tall] * 16, axis=0)
            values[side, o] = jnp.where(chosen, tall, 0.0).astype(bf16)
    order = [(side, o) for side in range(2) for o in range(owners)]
    mask = jnp.concatenate([masks[at] for at in order], axis=1)
    value = jnp.concatenate([values[at] for at in order], axis=1)
    out_ref[...] = dot_nt(mask, value) + channels
    mine = jnp.where(own_tm == 0.0, resid_owner[0], resid_owner[1])
    quarter = resid_ref.shape[1]
    part = mine[:, 0:quarter]
    for q in range(1, NPOL):
        part = jnp.where(own_pol[:, 0:quarter] == float(q), mine[:, q * quarter : (q + 1) * quarter], part)
    resid_ref[...] = part


def gradient_rows(info, got):
    vmem = pl.BlockSpec(memory_space=pltpu.VMEM)
    return pl.pallas_call(
        gradient_kernel,
        out_shape=(
            pltpu.VMEM((2 * NPOL, VT // NPOL), f32),
            pltpu.VMEM((NST // 8, 128), f32),
        ),
        in_specs=[vmem, vmem],
        out_specs=(vmem, vmem),
        compiler_params=pltpu.CompilerParams(vmem_limit_bytes=12 * MIB),
        cost_estimate=pl.CostEstimate(flops=70_000_000, bytes_accessed=MIB, transcendentals=0),
        name="gradient",
    )(info, got)


def collect_kernel(got_ref, mine_ref, out_hbm, resid_hbm, out_ref, resid_ref, sem):
    turned = got_ref[...].T
    lanes = 2 * turned.shape[1]
    channel_row = lax.broadcasted_iota(jnp.int32, (128, lanes), 0) >> 2
    group_row = lax.broadcasted_iota(jnp.int32, (8, lanes), 0)
    values = []
    groups = []
    for block in range(NBLK):
        pair = (block, block + NBLK)
        channel = jnp.concatenate([turned[64 + b : 65 + b] for b in pair], axis=1).astype(jnp.int32)
        terms = jnp.concatenate([turned[4 * b : 4 * b + 4] for b in pair], axis=1)
        tall = jnp.concatenate([terms, terms], axis=0)
        tall = jnp.concatenate([tall] * 16, axis=0)
        value = jnp.where(channel_row == (channel & 31), tall, 0.0).astype(bf16)
        group = jnp.where(group_row == (channel >> 5), 1.0, 0.0).astype(bf16)
        values.append(value)
        groups.append(group)
    total = dot_nt(jnp.concatenate(groups, axis=1), jnp.concatenate(values, axis=1))
    out_ref[...] = grad_scale * total
    out_copy = pltpu.make_async_copy(out_ref, out_hbm, sem.at[1])
    out_copy.start()
    part = mine_ref[...]
    for row in range(2 * NPOL):
        resid_ref[0, row] = part[row : row + 1, :]
    resid_copy = pltpu.make_async_copy(resid_ref, resid_hbm, sem.at[0])
    resid_copy.start()
    out_copy.wait()
    resid_copy.wait()


def collect_rows(got, mine, quarter):
    vmem = pl.BlockSpec(memory_space=pltpu.VMEM)
    return pl.pallas_call(
        collect_kernel,
        out_shape=(
            jax.ShapeDtypeStruct((8, 128), f32),
            jax.ShapeDtypeStruct((1, 2 * NPOL, 1, quarter), f32),
        ),
        in_specs=[vmem, vmem],
        out_specs=(pl.BlockSpec(memory_space=pl.ANY),) * 2,
        scratch_shapes=[
            pltpu.VMEM((8, 128), f32),
            pltpu.VMEM((1, 2 * NPOL, 1, quarter), f32),
            pltpu.SemaphoreType.DMA((2,)),
        ],
        compiler_params=pltpu.CompilerParams(vmem_limit_bytes=8 * MIB),
        cost_estimate=pl.CostEstimate(flops=2_000_000, bytes_accessed=65536, transcendentals=0),
        name="collect",
    )(got, mine)


def on_device(
    tile_spectral_lines,
    taper_leading_axis,
    taper_trailing_axis,
    depth_layer_factors,
    measured_correlations,
    visibility_groups_table,
    antenna_links,
    complex_receiver_factors,
):
    where = jnp.stack([lax.axis_index("facet"), lax.axis_index("pol"), lax.axis_index("tm")]).astype(jnp.int32)
    quarter = measured_correlations.shape[3]
    u = taper_leading_axis.reshape(VT, SG)
    v = taper_trailing_axis.reshape(VT, SG)
    w = depth_layer_factors.reshape(NW, VT)
    x = tile_spectral_lines.reshape(tile_spectral_lines.shape[2:])
    contrib, pack = contributions(x, u, v, w)
    received = lax.all_to_all(contrib, "facet", split_axis=0, concat_axis=0, tiled=True)
    other = lax.ppermute(pack, "tm", [(0, 1), (1, 0)])
    b, a = taper_transforms(where, pack, other)
    info = slot_rows(
        where,
        visibility_groups_table.reshape(3, NBLK),
        measured_correlations,
        antenna_links,
        complex_receiver_factors,
    )
    peers = lax.axis_size(("pol", "tm"))
    sent = partial_predictions(received, b, a, info, peers)
    gathered = lax.all_to_all(sent, ("pol", "tm"), split_axis=0, concat_axis=0, tiled=True)
    mine, partial_rows = gradient_rows(info, gathered)
    rows = lax.all_to_all(
        partial_rows.reshape(NST // 8, 1, 128), "facet", split_axis=0, concat_axis=0, tiled=True
    )
    gain_grad, residual = collect_rows(rows.reshape(NST // 8, 128), mine, quarter)
    return (residual, gain_grad.reshape(1, 4 * NCH))


def solution(mesh):
    return jax.shard_map(
        on_device,
        mesh=mesh,
        in_specs=(
            P("facet", "pol", None, "tm", None),
            P("facet", "tm", None, None),
            P("facet", "tm", None, None),
            P("facet", "tm", None, None),
            P("facet", None, "tm", "pol"),
            P("facet", "tm", None, None),
            P(),
            P(),
        ),
        out_specs=(P("facet", None, "tm", "pol"), P(("facet", "pol", "tm"), None)),
        check_vma=False,
    )
```
